32 devices in a mesh: dp: 4 (over y, x), expert: 8 (over z, core).
Axes of the slice: x: 2, y: 2, z: 4, core: 2. Of those that a mesh axis runs over, the one named last changes fastest.
Arguments:
- tokens: bfloat16 [4096, 2048], P(('dp', 'expert')), may hold values from -6 to 6
- expert_ids: int32 [4096, 8], P(('dp', 'expert')), may hold values from 0 to 15, all different within a row
- bucket_codes: int32 [4096, 8], P(('dp', 'expert')), may hold values from 0 to 65535
- route_weights: float32 [4096, 8], P(('dp', 'expert')), may hold values from 0.1 to 1
- cotangent: bfloat16 [4096, 2048], P(('dp', 'expert')), may hold values from -2 to 2
- counts: int32 [16], replicated, may hold values from 4 to 16, as said below
- comp_scale: bfloat16 [16, 2048], replicated, may hold values from -3 to 3
- w_gate: bfloat16 [16, 2048, 768], P('expert'), may hold values from -0.125 to 0.125
- w_up: bfloat16 [16, 2048, 768], P('expert'), may hold values from -0.125 to 0.125
- w_down: bfloat16 [16, 768, 2048], P('expert'), may hold values from -0.21875 to 0.21875
Outputs:
- layer_output: bfloat16 [4096, 2048], P(('dp', 'expert'))
- grad_tokens: bfloat16 [4096, 2048], P(('dp', 'expert'))
- grad_down: bfloat16 [16, 768, 2048], P('expert', None, 'dp')
The draws below stay inside these ranges and needn't reach their ends.
Inputs may be any that keep to these rules, and one draw needn't show every extreme that they name: `counts`: experts 2i and 2i+1 (those of index i of the expert axis) have 20 buckets together; some expert has exactly 16. `expert_ids`: the 8 experts of one token differ.
All inputs are finite; a program needn't handle non-finite values.
Results may differ from the reference program's by a relative error of at most 0.013.
Values may be sent and summed in bfloat16 or wider, within the bound.
No kernel may reach another device: no remote copies, remote signals or barrier semaphores. Data moves between devices by JAX's collectives and lax.ppermute only.
A program may use at most 192 MiB of HBM per device.

```python
import jax
import jax.numpy as jnp
from jax import lax

D = 2048
FF = 768
TOPK = 8
NB = 16
BUCKET_DEV = 20
TOK_DEV = 128
EXPERTS = 16
TOKENS = 4096
N_DP = 4
N_EXPERT = 8


def draw_counts(key, part):
    half_total = EXPERTS // 2
    first_key = jax.random.fold_in(key, 11)
    pick_key = jax.random.fold_in(key, 12)
    first_count = jax.random.randint(first_key, (half_total,), BUCKET_DEV - NB, NB + 1, dtype=jnp.int32)
    chosen = jax.random.randint(pick_key, (), 0, half_total, dtype=jnp.int32)
    first_count = jnp.where(jnp.arange(half_total, dtype=jnp.int32) == chosen, NB, first_count)
    second_count = BUCKET_DEV - first_count
    return jnp.stack([first_count, second_count], axis=1).reshape(EXPERTS).astype(jnp.int32)


def with_ends(values, rng, least, high):
    longest = values.shape.index(max(values.shape))
    spots = []
    for shift in (0, 1):
        where = [jax.random.randint(jax.random.fold_in(rng, axis), (), 0, length) for axis, length in enumerate(values.shape)]
        where[longest] = (where[longest] + shift) % values.shape[longest]
        spots.append(tuple(where))
    return values.at[spots[0]].set(least).at[spots[1]].set(high)


def block_scale(rng, shape, pieces, least, high):
    level = 1.0
    for dim, parts in pieces:
        draws = jax.random.uniform(jax.random.fold_in(jax.random.fold_in(rng, 6), dim), (parts,), jnp.float32, least / len(pieces), high / len(pieces))
        level = level * jnp.repeat(jnp.exp(draws), shape[dim] // parts).reshape((-1,) + (1,) * (len(shape) - 1 - dim))
    return level


def choose_distinct(own_key, rows, count, top, lift):
    ranking = jax.random.permutation(jax.random.fold_in(own_key, 1), count)
    favour = ranking
    for power in range(3):
        favour = favour * favour // count
    favour = favour * lift // count
    chance = jax.random.randint(jax.random.fold_in(own_key, 2), (rows, count), 0, 4096) + favour
    fixed_rows = jax.random.permutation(jax.random.fold_in(own_key, 3), rows)[jnp.arange(count) % rows]
    chance = jnp.where(jnp.arange(rows)[:, None] == fixed_rows[None, :], 1 << 14, chance)
    score = chance * count + jnp.arange(count)
    return lax.top_k(score.astype(jnp.int32), top)[1].astype(jnp.int32)


def normal_values(rng, shape, scale, most, cuts=(), kind=jnp.bfloat16):
    array = scale * jax.random.normal(rng, shape, jnp.float32)
    if cuts:
        array = array * block_scale(rng, shape, cuts, -0.22, 0.18)
    return jnp.clip(array, -most, most).astype(kind)


def setup_inputs(seed: int = 0) -> dict:
    arg_keys = jax.random.split(jax.random.key(seed), 11)
    tokens = normal_values(arg_keys[0], (TOKENS, D), 1.0, 6.0, ((0, 32),))
    expert_ids = choose_distinct(arg_keys[1], TOKENS, EXPERTS, TOPK, 8192)
    bucket_codes = with_ends(jax.random.randint(arg_keys[2], (TOKENS, TOPK), 0, 65536), jax.random.fold_in(arg_keys[2], 1), 0, 65535).astype(jnp.int32)
    route_weights = jnp.clip(0.1 + 0.9 * jax.random.uniform(arg_keys[3], (TOKENS, TOPK), jnp.float32) ** block_scale(arg_keys[3], (TOKENS, TOPK), ((0, 32),), -0.2, 0.2), 0.1, 1.0)
    cotangent = normal_values(arg_keys[4], (TOKENS, D), 0.3, 2.0, ((0, 32),))
    counts = draw_counts(jax.random.fold_in(arg_keys[10], 71), 0)
    comp_scale = normal_values(arg_keys[6], (EXPERTS, D), 0.5, 3.0)
    w_gate = normal_values(arg_keys[7], (EXPERTS, D, FF), D ** -0.5, 0.125, ((0, 8),))
    w_up = normal_values(arg_keys[8], (EXPERTS, D, FF), D ** -0.5, 0.125, ((0, 8),))
    w_down = normal_values(arg_keys[9], (EXPERTS, FF, D), FF ** -0.5, 0.21875, ((0, 8),))
    return {"tokens": tokens, "expert_ids": expert_ids, "bucket_codes": bucket_codes, "route_weights": route_weights, "cotangent": cotangent, "counts": counts, "comp_scale": comp_scale, "w_gate": w_gate, "w_up": w_up, "w_down": w_down}


def reference(tokens, expert_ids, bucket_codes, route_weights, cotangent, counts, comp_scale, w_gate, w_up, w_down):
    sources = N_DP * N_EXPERT
    slot_total = EXPERTS * NB
    tok_blocks = tokens.reshape(sources, TOK_DEV, D)
    id_blocks = expert_ids.reshape(sources, TOK_DEV, TOPK)
    code_blocks = bucket_codes.reshape(sources, TOK_DEV, TOPK)
    weight_blocks = route_weights.reshape(sources, TOK_DEV, TOPK)
    cot_blocks = cotangent.reshape(sources, TOK_DEV, D)

    def slot_of(id_block, code_block):
        pair_count = counts[id_block]
        return (id_block * NB + code_block % pair_count).astype(jnp.int32)

    def build(block):
        tok_block, id_block, code_block, weight_block, cot_block = block
        slot_id = slot_of(id_block, code_block)
        slot_hit = (slot_id[:, :, None] == jnp.arange(slot_total, dtype=jnp.int32)).astype(jnp.float32)
        member = jnp.sum(slot_hit, axis=1).T
        weighted = jnp.sum(slot_hit * weight_block[:, :, None], axis=1).T
        occupancy = jnp.sum(member, axis=1)
        bucket_sums = jnp.dot(member, tok_block.astype(jnp.float32), precision=lax.Precision.HIGHEST)
        centroid = (bucket_sums / jnp.maximum(occupancy, 1.0)[:, None]).astype(jnp.bfloat16)
        pull_sum = jnp.dot(weighted, cot_block.astype(jnp.float32), precision=lax.Precision.HIGHEST).astype(jnp.bfloat16)
        return centroid, pull_sum, occupancy

    centroids, pulls, occupancies = lax.map(build, (tok_blocks, id_blocks, code_blocks, weight_blocks, cot_blocks))
    cent_four = centroids.reshape(sources, EXPERTS, NB, D)
    pull_four = pulls.reshape(sources, EXPERTS, NB, D)

    def expert_step(index):
        arrived = lax.dynamic_index_in_dim(cent_four, index, axis=1, keepdims=False).reshape(sources * NB, D)
        pull_rows = lax.dynamic_index_in_dim(pull_four, index, axis=1, keepdims=False).reshape(sources * NB, D)
        gate_weight = lax.dynamic_index_in_dim(w_gate, index, axis=0, keepdims=False)
        up_weight = lax.dynamic_index_in_dim(w_up, index, axis=0, keepdims=False)
        down_weight = lax.dynamic_index_in_dim(w_down, index, axis=0, keepdims=False)
        gate_act = jnp.dot(arrived, gate_weight, preferred_element_type=jnp.float32)
        up_act = jnp.dot(arrived, up_weight, preferred_element_type=jnp.float32)
        gate_sigmoid = jax.nn.sigmoid(gate_act)
        hidden = (gate_act * gate_sigmoid * up_act).astype(jnp.bfloat16)
        expert_out = jnp.dot(hidden, down_weight, preferred_element_type=jnp.float32).astype(jnp.bfloat16)
        d_hidden = jnp.dot(pull_rows, down_weight.T, preferred_element_type=jnp.float32)
        d_gate = (d_hidden * up_act * gate_sigmoid * (1.0 + gate_act * (1.0 - gate_sigmoid))).astype(jnp.bfloat16)
        d_up = (d_hidden * gate_act * gate_sigmoid).astype(jnp.bfloat16)
        back_rows = (jnp.dot(d_gate, gate_weight.T, preferred_element_type=jnp.float32)
                     + jnp.dot(d_up, up_weight.T, preferred_element_type=jnp.float32)).astype(jnp.bfloat16)
        hidden_groups = hidden.reshape(N_DP, N_EXPERT * NB, FF).astype(jnp.float32)
        pull_groups = pull_rows.reshape(N_DP, N_EXPERT * NB, D).astype(jnp.float32)
        partial_grad = jnp.einsum("pqf,pqd->pfd", hidden_groups, pull_groups, precision=lax.Precision.HIGHEST)
        rounded = lax.optimization_barrier(partial_grad.astype(jnp.bfloat16)).astype(jnp.float32)
        grad_expert = jnp.sum(rounded, axis=0).astype(jnp.bfloat16)
        return expert_out.reshape(sources, NB, D), back_rows.reshape(sources, NB, D), grad_expert

    outs, backs, grad_down = lax.map(expert_step, jnp.arange(EXPERTS, dtype=jnp.int32))
    out_blocks = jnp.transpose(outs, (1, 0, 2, 3)).reshape(sources, slot_total, D)
    back_blocks = jnp.transpose(backs, (1, 0, 2, 3)).reshape(sources, slot_total, D)

    def combine(block):
        tok_block, id_block, code_block, weight_block, cot_block, cent_block, pull_block, out_block, back_block, occ_block = block
        slot_id = slot_of(id_block, code_block)
        out_pair = out_block[slot_id].astype(jnp.float32)
        cent_pair = cent_block[slot_id].astype(jnp.float32)
        pull_pair = pull_block[slot_id].astype(jnp.float32)
        back_pair = back_block[slot_id].astype(jnp.float32)
        occ_pair = jnp.maximum(occ_block[slot_id], 1.0)
        scale_pair = comp_scale[id_block].astype(jnp.float32)
        route_pair = weight_block[:, :, None]
        layer = jnp.sum(route_pair * (out_pair + scale_pair * (tok_block.astype(jnp.float32)[:, None, :] - cent_pair)), axis=1)
        grad_tok = jnp.sum(route_pair * scale_pair * cot_block.astype(jnp.float32)[:, None, :]
                           + (back_pair - scale_pair * pull_pair) / occ_pair[:, :, None], axis=1)
        return layer.astype(jnp.bfloat16), grad_tok.astype(jnp.bfloat16)

    layers, grads = lax.map(combine, (tok_blocks, id_blocks, code_blocks, weight_blocks, cot_blocks,
                                      centroids, pulls, out_blocks, back_blocks, occupancies))
    return layers.reshape(TOKENS, D), grads.reshape(TOKENS, D), grad_down
```

```python
import functools

import jax
import jax.numpy as jnp
from jax import lax
from jax.experimental import pallas as pl
from jax.experimental.pallas import tpu as pltpu
from jax.sharding import PartitionSpec as P

PAIR_ROWS = 20
HALVES = 2
BLOCK_ROWS = HALVES * PAIR_ROWS
CHUNK = 8
FF_TILE = 256
VMEM_LIMIT = 48 * 1024 * 1024
F32 = jnp.float32
BF16 = jnp.bfloat16

NN = (((1,), (0,)), ((), ()))
NT = (((1,), (1,)), ((), ()))
TN = (((0,), (0,)), ((), ()))


def mm(a, b, dims=NN):
    return lax.dot_general(a, b, dims, preferred_element_type=F32)


def iota(shape, dim):
    return lax.broadcasted_iota(jnp.int32, shape, dim)


def over_pair_rows(index):
    return jnp.floor((index.astype(F32) + 0.5) * (1.0 / PAIR_ROWS)).astype(jnp.int32)


def pair_rows_of(ids, codes, counts_ref, group):
    count = jnp.zeros_like(ids)
    base = jnp.zeros_like(ids)
    for expert in range(counts_ref.shape[0]):
        hit = ids == expert
        count = jnp.where(hit, counts_ref[expert], count)
        if expert % 2:
            base = jnp.where(hit, counts_ref[expert - 1], base)
    laps = jnp.floor((codes.astype(F32) + 0.5) / count.astype(F32)).astype(jnp.int32)
    bucket = codes - laps * count
    return ((ids >> 1) ^ group) * BLOCK_ROWS + base + bucket


def membership(rows, total, values):
    picks, tokens = rows.shape
    index = iota((total, tokens), 0)
    parts = []
    for half in range(HALVES):
        part = jnp.zeros((total, tokens), F32)
        for pick in range(picks):
            hit = index == rows[pick : pick + 1, :] + half * PAIR_ROWS
            value = 1.0 if values is None else values[pick : pick + 1, :]
            part = jnp.where(hit, value, part)
        parts.append(part)
    return jnp.concatenate(parts, axis=1)


def split_halves(x):
    width = x.shape[1] // HALVES
    return jnp.concatenate([x[:, :width], x[:, width:]], axis=0)


def unpack_rows(blocks):
    flat = jnp.concatenate([b[...] for b in blocks], axis=0)
    rows = len(blocks) * PAIR_ROWS
    shape = (rows, len(blocks) * BLOCK_ROWS)
    row = iota(shape, 0)
    start = row + PAIR_ROWS * over_pair_rows(row)
    col = iota(shape, 1)
    out = []
    for half in range(HALVES):
        pick = (col == start + half * PAIR_ROWS).astype(F32).astype(BF16)
        out.append(mm(pick, flat).astype(BF16))
    return jnp.concatenate(out, axis=1)


def pack_rows(x, blocks):
    rows = len(blocks) * PAIR_ROWS
    total = len(blocks) * BLOCK_ROWS
    row = iota((total, rows), 0)
    col = iota((total, rows), 1)
    start = col + PAIR_ROWS * over_pair_rows(col)
    pick = jnp.concatenate(
        [(row == start + half * PAIR_ROWS).astype(F32) for half in range(HALVES)], axis=1
    ).astype(BF16)
    out = mm(pick, split_halves(x))
    for j, block in enumerate(blocks):
        block[...] = out[j * BLOCK_ROWS : (j + 1) * BLOCK_ROWS].astype(BF16)


def first_rows(rows, counts_ref, group):
    index = iota((rows, 1), 0)
    inside = index - PAIR_ROWS * over_pair_rows(index)
    return inside < counts_ref[2 * group]


def gather_kernel(mean, counts_ref, group_ref, ids_ref, codes_ref, weights_ref, x_ref, *outs):
    rows = pair_rows_of(ids_ref[...], codes_ref[...], counts_ref, group_ref[0])
    total = len(outs) * BLOCK_ROWS
    member = membership(rows, total, None if mean else weights_ref[...])
    sums = mm(member.astype(BF16), split_halves(x_ref[...]))
    if mean:
        occupancy = jnp.sum(member, axis=1, keepdims=True)
        sums = sums / jnp.maximum(occupancy, 1.0)
    for j, out in enumerate(outs):
        out[...] = sums[j * BLOCK_ROWS : (j + 1) * BLOCK_ROWS].astype(BF16)


def spread_kernel(mean, counts_ref, group_ref, ids_ref, codes_ref, weights_ref, x_ref, scale_ref, *refs):
    blocks, out_ref = refs[:-1], refs[-1]
    ids = ids_ref[...]
    weights = weights_ref[...]
    experts, width = scale_ref.shape
    tokens = ids.shape[1]
    expert = iota((experts, tokens), 0)
    mix = jnp.zeros((experts, tokens), F32)
    for pick in range(ids.shape[0]):
        mix = jnp.where(expert == ids[pick : pick + 1, :], weights[pick : pick + 1, :], mix)
    high = mix.astype(BF16)
    low = (mix - high.astype(F32)).astype(BF16)
    scale = scale_ref[...]
    gain = mm(high, scale, TN) + mm(low, scale, TN)
    base = gain * x_ref[...].astype(F32)
    rows = pair_rows_of(ids, codes_ref[...], counts_ref, group_ref[0])
    total = len(blocks) * BLOCK_ROWS
    member = membership(rows, total, None if mean else weights)
    if mean:
        occupancy = jnp.sum(member, axis=1, keepdims=True)
        member = member / jnp.maximum(occupancy, 1.0)
    flat = jnp.concatenate([b[...] for b in blocks], axis=0)
    back = mm(member.astype(BF16), flat, TN)
    half = width // HALVES
    for h in range(HALVES):
        cols = slice(h * half, (h + 1) * half)
        out_ref[:, cols] = (base[:, cols] + back[h * tokens : (h + 1) * tokens]).astype(BF16)


def forward_kernel(n, counts_ref, group_ref, scale_ref, wg_ref, wu_ref, wd_ref, *refs):
    blocks, outs = refs[:n], refs[n : 2 * n]
    hidden_ref, slope_ref, silu_ref, x_ref, acc_ref = refs[2 * n :]
    e, f = pl.program_id(0), pl.program_id(1)
    rows = n * PAIR_ROWS

    @pl.when((e == 0) & (f == 0))
    def _():
        for c in range(0, n, CHUNK):
            part = blocks[c : c + CHUNK]
            x_ref[c * PAIR_ROWS : (c + len(part)) * PAIR_ROWS, :] = unpack_rows(part)
        acc_ref[...] = jnp.zeros_like(acc_ref)

    x = x_ref[...]
    gate = mm(x, wg_ref[0])
    up = mm(x, wu_ref[0])
    sg = 1.0 / (1.0 + jnp.exp(-gate))
    silu = gate * sg
    first = first_rows(rows, counts_ref, group_ref[0])
    mine = first == (e == 0)
    hidden = jnp.where(mine, silu * up, 0.0).astype(BF16)
    slope = jnp.where(mine, up * sg * (1.0 + gate * (1.0 - sg)), 0.0)
    silu = jnp.where(mine, silu, 0.0)
    acc_ref[...] += mm(hidden, wd_ref[0])
    tile = hidden.shape[1]
    cols = pl.ds(pl.multiple_of(f * tile, tile), tile)

    @pl.when(e == 0)
    def _():
        hidden_ref[:, cols] = hidden
        slope_ref[:, cols] = slope
        silu_ref[:, cols] = silu

    @pl.when(e == 1)
    def _():
        hidden_ref[:, cols] += hidden
        slope_ref[:, cols] += slope
        silu_ref[:, cols] += silu

    @pl.when((e == pl.num_programs(0) - 1) & (f == pl.num_programs(1) - 1))
    def _():
        scale = jnp.where(first, scale_ref[0, 0:1, :].astype(F32), scale_ref[0, 1:2, :].astype(F32))
        out = (acc_ref[...] - scale * x_ref[...].astype(F32)).astype(BF16)
        for c in range(0, n, CHUNK):
            part = outs[c : c + CHUNK]
            pack_rows(out[c * PAIR_ROWS : (c + len(part)) * PAIR_ROWS], part)


def unpack_kernel(n, parts, dp_ref, *refs):
    blocks, pull_ref, shares = refs[:n], refs[n], refs[n + 1 :]
    for c in range(0, n, CHUNK):
        part = blocks[c : c + CHUNK]
        pull_ref[c * PAIR_ROWS : (c + len(part)) * PAIR_ROWS, :] = unpack_rows(part)
    width = pull_ref.shape[1] // parts
    for k, share in enumerate(shares):
        start = pl.multiple_of((dp_ref[0] ^ k) * width, width)
        share[...] = pull_ref[:, pl.ds(start, width)]


def backward_kernel(n, counts_ref, group_ref, scale_ref, wg_ref, wu_ref, wd_ref, pull_ref, slope_ref, silu_ref, *refs):
    outs, acc_ref = refs[:n], refs[n]
    e, f = pl.program_id(0), pl.program_id(1)
    rows = n * PAIR_ROWS

    @pl.when((e == 0) & (f == 0))
    def _():
        acc_ref[...] = jnp.zeros_like(acc_ref)

    first = first_rows(rows, counts_ref, group_ref[0])
    mine = first == (e == 0)
    tile = wg_ref.shape[2]
    cols = pl.ds(pl.multiple_of(f * tile, tile), tile)
    d_hidden = jnp.where(mine, mm(pull_ref[...], wd_ref[0], NT), 0.0)
    d_gate = (d_hidden * slope_ref[:, cols]).astype(BF16)
    d_up = (d_hidden * silu_ref[:, cols]).astype(BF16)
    acc_ref[...] += mm(d_gate, wg_ref[0], NT) + mm(d_up, wu_ref[0], NT)

    @pl.when((e == pl.num_programs(0) - 1) & (f == pl.num_programs(1) - 1))
    def _():
        scale = jnp.where(first, scale_ref[0, 0:1, :].astype(F32), scale_ref[0, 1:2, :].astype(F32))
        out = (acc_ref[...] - scale * pull_ref[...].astype(F32)).astype(BF16)
        for c in range(0, n, CHUNK):
            part = outs[c : c + CHUNK]
            pack_rows(out[c * PAIR_ROWS : (c + len(part)) * PAIR_ROWS], part)


def grad_kernel(parts, counts_ref, group_ref, *refs):
    hidden, shares, out_ref = refs[:parts], refs[parts : 2 * parts], refs[2 * parts]
    rows = hidden[0].shape[0]
    first = first_rows(rows, counts_ref, group_ref[0])
    h_all = jnp.concatenate([h[...] for h in hidden], axis=0)
    lane = []
    for keep in (first, jnp.logical_not(first)):
        lane.append(
            jnp.concatenate(
                [jnp.where(keep, s[...].astype(F32), 0.0).astype(BF16) for s in shares], axis=0
            )
        )
    for e in range(2):
        out_ref[e] = mm(h_all, lane[e], TN).astype(BF16)


SMEM = pl.BlockSpec(memory_space=pltpu.SMEM)
VMEM = pl.BlockSpec(memory_space=pltpu.VMEM)


def call(kernel, n_smem, n_vmem, outs, flops, nbytes):
    return pl.pallas_call(
        kernel,
        out_shape=outs,
        in_specs=[SMEM] * n_smem + [VMEM] * n_vmem,
        out_specs=jax.tree.map(lambda _: VMEM, outs),
        compiler_params=pltpu.CompilerParams(vmem_limit_bytes=VMEM_LIMIT),
        cost_estimate=pl.CostEstimate(flops=flops, bytes_accessed=nbytes, transcendentals=0),
    )


def on_device(
    tokens, expert_ids, bucket_codes, route_weights, cotangent, counts, comp_scale, w_gate, w_up, w_down
):
    tok_count, width = tokens.shape
    n = lax.axis_size("expert")
    parts = lax.axis_size("dp")
    ff = w_gate.shape[2]
    half = width // HALVES
    rows = n * PAIR_ROWS
    total = n * BLOCK_ROWS
    group = lax.axis_index("expert").astype(jnp.int32).reshape(1)
    dp = lax.axis_index("dp").astype(jnp.int32).reshape(1)
    ids, codes, weights = expert_ids.T, bucket_codes.T, route_weights.T
    block = jax.ShapeDtypeStruct((BLOCK_ROWS, half), BF16)
    blocks = [block] * n
    block_bytes = total * width

    def exchange(values):
        return [values[0]] + [
            lax.ppermute(values[k], "expert", [(i, i ^ k) for i in range(n)]) for k in range(1, n)
        ]

    def exchange_dp(values):
        return [values[0]] + [
            lax.ppermute(values[k], "dp", [(i, i ^ k) for i in range(parts)]) for k in range(1, parts)
        ]

    def gather(mean, x):
        return call(
            functools.partial(gather_kernel, mean), 2, 4, blocks, 2 * total * tok_count * width, block_bytes
        )(counts, group, ids, codes, weights, x)

    def spread(mean, x, got):
        return call(
            functools.partial(spread_kernel, mean),
            2,
            5 + n,
            jax.ShapeDtypeStruct(tokens.shape, BF16),
            2 * total * tok_count * width,
            block_bytes,
        )(counts, group, ids, codes, weights, x, comp_scale, *got)

    sent_c = gather(True, tokens)
    got_c = exchange(sent_c)
    sent_p = gather(False, cotangent)
    got_p = exchange(sent_p)

    local = w_gate.shape[0]
    scale_three = comp_scale.reshape(n, local, width)
    tile_grid = (local, ff // FF_TILE)
    whole = lambda shape: pl.BlockSpec(shape, lambda e, f: (0,) * len(shape))
    scale_spec = pl.BlockSpec((1, local, width), lambda e, f: (0, 0, 0))
    own_scale = lax.dynamic_slice_in_dim(scale_three, group[0], 1, axis=0)
    weight_specs = [
        pl.BlockSpec((1, width, FF_TILE), lambda e, f: (e, 0, f)),
        pl.BlockSpec((1, width, FF_TILE), lambda e, f: (e, 0, f)),
        pl.BlockSpec((1, FF_TILE, width), lambda e, f: (e, f, 0)),
    ]
    weight_bytes = 3 * local * width * ff * 2
    expert_flops = 2 * 3 * rows * local * width * ff
    params = pltpu.CompilerParams(
        vmem_limit_bytes=VMEM_LIMIT, dimension_semantics=("arbitrary", "arbitrary")
    )
    cost = pl.CostEstimate(flops=expert_flops, bytes_accessed=weight_bytes, transcendentals=rows * ff)

    results = pl.pallas_call(
        functools.partial(forward_kernel, n),
        grid=tile_grid,
        in_specs=[SMEM, SMEM, scale_spec] + weight_specs + [whole(block.shape)] * n,
        out_specs=[whole(block.shape)] * n + [whole((rows, ff))] * 3,
        out_shape=blocks
        + [
            jax.ShapeDtypeStruct((rows, ff), BF16),
            jax.ShapeDtypeStruct((rows, ff), F32),
            jax.ShapeDtypeStruct((rows, ff), F32),
        ],
        scratch_shapes=[pltpu.VMEM((rows, width), BF16), pltpu.VMEM((rows, width), F32)],
        compiler_params=params,
        cost_estimate=cost,
    )(counts, group, own_scale, w_gate, w_up, w_down, *got_c)
    sent_o, (hidden, slope, silu) = results[:n], results[n:]
    got_o = exchange(sent_o)
    all_hidden = exchange_dp([hidden] * parts)

    pull_and_shares = call(
        functools.partial(unpack_kernel, n, parts),
        1,
        n,
        [jax.ShapeDtypeStruct((rows, width), BF16)]
        + [jax.ShapeDtypeStruct((rows, width // parts), BF16)] * parts,
        2 * rows * min(n, CHUNK) * BLOCK_ROWS * width,
        2 * block_bytes,
    )(dp, *got_p)
    pull = pull_and_shares[0]
    all_shares = exchange_dp(pull_and_shares[1:])

    sent_b = pl.pallas_call(
        functools.partial(backward_kernel, n),
        grid=tile_grid,
        in_specs=[SMEM, SMEM, scale_spec]
        + weight_specs
        + [whole((rows, width)), whole((rows, ff)), whole((rows, ff))],
        out_specs=[whole(block.shape)] * n,
        out_shape=blocks,
        scratch_shapes=[pltpu.VMEM((rows, width), F32)],
        compiler_params=params,
        cost_estimate=cost,
    )(counts, group, own_scale, w_gate, w_up, w_down, pull, slope, silu)
    got_b = exchange(sent_b)

    grad_down = call(
        functools.partial(grad_kernel, parts),
        2,
        2 * parts,
        jax.ShapeDtypeStruct((local, ff, width // parts), BF16),
        2 * parts * rows * ff * local * width // parts,
        parts * rows * (ff + width // parts) * 2,
    )(counts, group, *all_hidden, *all_shares)
    layer_output = spread(False, tokens, got_o)
    grad_tokens = spread(True, cotangent, got_b)
    return (layer_output, grad_tokens, grad_down)


def solution(mesh):
    token_spec = P(("dp", "expert"), None)
    weight_spec = P("expert", None, None)
    in_specs = (token_spec,) * 5 + (P(), P()) + (weight_spec,) * 3
    out_specs = (token_spec, token_spec, P("expert", None, "dp"))
    return jax.shard_map(
        on_device, mesh=mesh, in_specs=in_specs, out_specs=out_specs, check_vma=False
    )
```

```python
import functools

import jax
import jax.numpy as jnp
from jax import lax
from jax.experimental import pallas as pl
from jax.experimental.pallas import tpu as pltpu
from jax.sharding import PartitionSpec as P

PAIR_ROWS = 20
MOST = 16
HALVES = 2
BLOCK_ROWS = HALVES * PAIR_ROWS
CHUNK = 8
FF_TILE = 256
VMEM_LIMIT = 64 * 1024 * 1024 - 65536
EXPERT_LIMIT = 64 * 1024 * 1024 - 65536
AHEAD = 4
TIE_O = True
TIE_L = True
TIE_P = ()
TIE_B = "hidden"
GATHER_HIDDEN = False
PREPARE_EARLY = True
TIE_G = True
WAY_C = "permute"
WAY_P = "permute"
WAY_O = "all"
WAY_B = "all"
F32 = jnp.float32
BF16 = jnp.bfloat16

NN = (((1,), (0,)), ((), ()))
NT = (((1,), (1,)), ((), ()))
TN = (((0,), (0,)), ((), ()))


def mm(a, b, dims=NN):
    return lax.dot_general(a, b, dims, preferred_element_type=F32)


def iota(shape, dim):
    return lax.broadcasted_iota(jnp.int32, shape, dim)


def pair_rows_of(ids, codes, counts_ref, group):
    count = jnp.zeros_like(ids)
    base = jnp.zeros_like(ids)
    for expert in range(counts_ref.shape[0]):
        hit = ids == expert
        count = jnp.where(hit, counts_ref[expert], count)
        if expert % 2:
            base = jnp.where(hit, counts_ref[expert - 1], base)
    laps = jnp.floor((codes.astype(F32) + 0.5) / count.astype(F32)).astype(jnp.int32)
    bucket = codes - laps * count
    return ((ids >> 1) ^ group) * BLOCK_ROWS + base + bucket


def membership(rows, total, values):
    picks, tokens = rows.shape
    index = iota((total, tokens), 0)
    parts = []
    for half in range(HALVES):
        part = jnp.zeros((total, tokens), F32)
        for pick in range(picks):
            hit = index == rows[pick : pick + 1, :] + half * PAIR_ROWS
            value = 1.0 if values is None else values[pick : pick + 1, :]
            part = jnp.where(hit, value, part)
        parts.append(part)
    return jnp.concatenate(parts, axis=1)


def split_halves(x):
    width = x.shape[1] // HALVES
    return jnp.concatenate([x[:, :width], x[:, width:]], axis=0)


def row_places(row, blocks):
    inside = jnp.floor((row.astype(F32) + 0.5) * (1.0 / blocks)).astype(jnp.int32)
    return (row - inside * blocks) * BLOCK_ROWS + inside


def unpack_rows(blocks):
    flat = jnp.concatenate(blocks, axis=0)
    count = len(blocks)
    shape = (count * PAIR_ROWS, count * BLOCK_ROWS)
    place = row_places(iota(shape, 0), count)
    col = iota(shape, 1)
    out = []
    for half in range(HALVES):
        pick = (col == place + half * PAIR_ROWS).astype(F32).astype(BF16)
        out.append(mm(pick, flat).astype(BF16))
    return jnp.concatenate(out, axis=1)


class Blocks:
    def __init__(self, refs, group):
        self.refs, self.group = refs, group

    def at(self, j):
        if len(self.refs) > 1:
            return self.refs[j]
        return self.refs[0].at[self.group ^ j]

    def load(self, start, stop):
        return [self.at(j)[...] for j in range(start, stop)]

    def store(self, start, flat):
        for j in range(flat.shape[0] // BLOCK_ROWS):
            self.at(start + j)[...] = flat[j * BLOCK_ROWS : (j + 1) * BLOCK_ROWS].astype(BF16)


def pack_windows(parts, n, c, size, counts_ref, group, dims):
    total = None
    for e, (x, (start, stop)) in enumerate(zip(parts, windows(n))):
        shape = (size * BLOCK_ROWS, stop - start)
        row = iota(shape, 0)
        index = iota(shape, 1) + start
        inside = jnp.floor((index.astype(F32) + 0.5) * (1.0 / n)).astype(jnp.int32)
        place = (index - inside * n - c) * BLOCK_ROWS + inside
        first = inside < counts_ref[2 * group]
        place = jnp.where(first if e == 0 else jnp.logical_not(first), place, -BLOCK_ROWS * n)
        if n > size:
            block = index - inside * n
            place = jnp.where((block >= c) & (block < c + size), place, -BLOCK_ROWS * n)
        picks = [(row == place + h * PAIR_ROWS).astype(F32).astype(BF16) for h in range(HALVES)]
        part = None
        half = x.shape[1 if dims == NN else 0] // HALVES
        for h, pick in enumerate(picks):
            piece = x[:, h * half : (h + 1) * half] if dims == NN else x[h * half : (h + 1) * half, :]
            product = mm(pick, piece, dims)
            part = product if part is None else part + product
        total = part if total is None else total + part
    return total


def windows(n):
    return (0, MOST * n), ((PAIR_ROWS - MOST) * n, PAIR_ROWS * n)


def owned(e, start, stop, n, counts_ref, group):
    index = iota((stop - start, 1), 0) + start
    first = index < counts_ref[2 * group] * n
    return first if e == 0 else jnp.logical_not(first)


def gather_kernel(mean, n, group_ref, counts_ref, ids_ref, codes_ref, weights_ref, x_ref, *outs):
    group = group_ref[0]
    rows = pair_rows_of(ids_ref[...], codes_ref[...], counts_ref, group)
    member = membership(rows, n * BLOCK_ROWS, None if mean else weights_ref[...])
    sums = mm(member.astype(BF16), split_halves(x_ref[...]))
    if mean:
        sums = sums / jnp.maximum(jnp.sum(member, axis=1, keepdims=True), 1.0)
    Blocks(outs, group).store(0, sums)


def own_scale(scale_ref, group, e):
    row = iota(scale_ref.shape, 0)
    return jnp.sum(jnp.where(row == 2 * group + e, scale_ref[...].astype(F32), 0.0), axis=0, keepdims=True)


def gain_of(ids, weights, scale):
    experts, tokens = scale.shape[0], ids.shape[1]
    expert = iota((experts, tokens), 0)
    mix = jnp.zeros((experts, tokens), F32)
    for pick in range(ids.shape[0]):
        mix = jnp.where(expert == ids[pick : pick + 1, :], weights[pick : pick + 1, :], mix)
    high = mix.astype(BF16)
    low = (mix - high.astype(F32)).astype(BF16)
    return mm(high, scale, TN) + mm(low, scale, TN)


def prepare_kernel(n, counts_ref, group_ref, ids_ref, codes_ref, weights_ref, tok_ref, cot_ref, scale_ref, *outs):
    base_l_ref, base_g_ref, mix_l_ref, mix_g_ref = outs
    ids = ids_ref[...]
    weights = weights_ref[...]
    gain = gain_of(ids, weights, scale_ref[...])
    base_l_ref[...] = gain * tok_ref[...].astype(F32)
    base_g_ref[...] = gain * cot_ref[...].astype(F32)
    rows = pair_rows_of(ids, codes_ref[...], counts_ref, group_ref[0])
    member = membership(rows, n * BLOCK_ROWS, None)
    divisor = jnp.maximum(jnp.sum(member, axis=1, keepdims=True), 1.0)
    mix_g_ref[...] = (member / divisor).T.astype(BF16)
    mix_l_ref[...] = membership(rows, n * BLOCK_ROWS, weights).T.astype(BF16)


def spread_kernel(n, group_ref, base_ref, mix_ref, *refs):
    blocks, out_ref = refs[:-1], refs[-1]
    flat = jnp.concatenate(Blocks(blocks, group_ref[0]).load(0, n), axis=0)
    back = mm(mix_ref[...], flat)
    tokens, width = out_ref.shape
    half = width // HALVES
    for h in range(HALVES):
        cols = slice(h * half, (h + 1) * half)
        out_ref[:, cols] = (base_ref[:, cols] + back[h * tokens : (h + 1) * tokens]).astype(BF16)


class Weights:
    def __init__(self, hbm, vmem, sems):
        self.hbm, self.vmem, self.sems = hbm, vmem, sems
        self.per = vmem[0].shape[2] // FF_TILE
        self.steps = vmem[0].shape[0] * self.per

    def views(self, s):
        e = s // self.per
        cols = pl.ds(pl.multiple_of((s - e * self.per) * FF_TILE, FF_TILE), FF_TILE)
        return [(e, slice(None), cols)] * 2 + [(e, cols, slice(None))]

    def copies(self, s):
        return [
            pltpu.make_async_copy(h.at[view], v.at[view], self.sems.at[s, i])
            for i, (h, v, view) in enumerate(zip(self.hbm, self.vmem, self.views(s)))
        ]

    def start(self, s):
        for copy in self.copies(s):
            copy.start()

    def run(self, body):
        for e in range(self.vmem[0].shape[0]):

            def step(f, carry):
                s = e * self.per + f

                @pl.when(s + AHEAD < self.steps)
                def _():
                    self.start(s + AHEAD)

                for copy in self.copies(s):
                    copy.wait()
                cols = pl.ds(pl.multiple_of(f * FF_TILE, FF_TILE), FF_TILE)
                body(e, cols, *[v.at[view] for v, view in zip(self.vmem, self.views(s))])
                return carry

            lax.fori_loop(0, self.per, step, 0)


def unpack_all(x_ref, blocks, n):
    size = min(CHUNK, n)
    for c in range(0, n, size):
        part = unpack_rows(blocks.load(c, c + size))
        if n == size:
            x_ref[...] = part
        else:
            for r in range(PAIR_ROWS):
                x_ref[r * n + c : r * n + c + size, :] = part[r * size : (r + 1) * size]


def forward_kernel(n, n_in, n_out, counts_ref, group_ref, scale_ref, wg_hbm, wu_hbm, wd_hbm, *refs):
    group = group_ref[0]
    blocks, outs = Blocks(refs[:n_in], group), Blocks(refs[n_in : n_in + n_out], group)
    hidden_ref, slope_ref, silu_ref, x_ref, acc_ref, wg_ref, wu_ref, wd_ref, sems = refs[n_in + n_out :]
    weights = Weights((wg_hbm, wu_hbm, wd_hbm), (wg_ref, wu_ref, wd_ref), sems)
    for s in range(AHEAD):
        weights.start(s)
    unpack_all(x_ref, blocks, n)
    hidden_ref[...] = jnp.zeros_like(hidden_ref)
    for e, (start, stop) in enumerate(windows(n)):
        scale = own_scale(scale_ref, group, e)
        acc_ref[e] = -(scale * x_ref[start:stop, :].astype(F32))

    def body(e, cols, wg, wu, wd):
        start, stop = windows(n)[e]
        mine = owned(e, start, stop, n, counts_ref, group)
        x = x_ref[start:stop, :]
        gate = mm(x, wg[...])
        up = mm(x, wu[...])
        sg = 1.0 / (1.0 + jnp.exp(-gate))
        silu = gate * sg
        hidden = (silu * up).astype(BF16)
        slope = up * sg * (1.0 + gate * (1.0 - sg))
        acc_ref[e] += mm(hidden, wd[...])
        hidden_ref[start:stop, cols] = jnp.where(mine, hidden, hidden_ref[start:stop, cols])
        slope_ref[e, cols, :] = slope.T
        silu_ref[e, cols, :] = silu.T

    weights.run(body)
    size = min(n, CHUNK)
    parts = [acc_ref[e].astype(BF16) for e in range(2)]
    for c in range(0, n, size):
        outs.store(c, pack_windows(parts, n, c, size, counts_ref, group, NN))


def unpack_kernel(n, n_in, parts, dp_ref, group_ref, *refs):
    blocks, pull_ref, shares = Blocks(refs[:n_in], group_ref[0]), refs[n_in], refs[n_in + 1 :]
    unpack_all(pull_ref, blocks, n)
    width = pull_ref.shape[1] // parts
    for k, share in enumerate(shares):
        start = pl.multiple_of((dp_ref[0] ^ k) * width, width)
        share[...] = pull_ref[:, pl.ds(start, width)]


def backward_kernel(n, n_out, counts_ref, group_ref, scale_ref, wg_hbm, wu_hbm, wd_hbm, pull_ref, slope_ref, silu_ref, *refs):
    group = group_ref[0]
    outs = Blocks(refs[:n_out], group)
    turned_ref, acc_ref, wg_ref, wu_ref, wd_ref, sems = refs[n_out:]
    weights = Weights((wg_hbm, wu_hbm, wd_hbm), (wg_ref, wu_ref, wd_ref), sems)
    for s in range(AHEAD):
        weights.start(s)
    for e, (start, stop) in enumerate(windows(n)):
        pull = pull_ref[start:stop, :].astype(F32)
        turned_ref[e] = pull.T.astype(BF16)
        acc_ref[e] = -(own_scale(scale_ref, group, e) * pull).T

    def body(e, cols, wg, wu, wd):
        d_hidden = mm(wd[...], turned_ref[e])
        d_gate = (d_hidden * slope_ref[e, cols, :]).astype(BF16)
        d_up = (d_hidden * silu_ref[e, cols, :]).astype(BF16)
        acc_ref[e] += mm(wg[...], d_gate) + mm(wu[...], d_up)

    weights.run(body)
    size = min(n, CHUNK)
    parts = [acc_ref[e].astype(BF16) for e in range(2)]
    for c in range(0, n, size):
        outs.store(c, pack_windows(parts, n, c, size, counts_ref, group, NT))


def grad_kernel(n, parts, counts_ref, group_ref, dp_ref, *refs):
    if GATHER_HIDDEN:
        hidden = [refs[0].at[dp_ref[0] ^ k] for k in range(parts)]
    else:
        hidden = refs[:parts]
    shares, out_ref = refs[-1 - parts : -1], refs[-1]
    for e in range(2):
        start, stop = windows(n)[e]
        mine = owned(e, start, stop, n, counts_ref, group_ref[0])
        h_all = jnp.concatenate([h[start:stop, :] for h in hidden], axis=0)
        pull = jnp.concatenate(
            [jnp.where(mine, s[start:stop, :].astype(F32), 0.0).astype(BF16) for s in shares], axis=0
        )
        out_ref[e] = mm(h_all, pull, TN).astype(BF16)


SMEM = pl.BlockSpec(memory_space=pltpu.SMEM)
VMEM = pl.BlockSpec(memory_space=pltpu.VMEM)
HBM = pl.BlockSpec(memory_space=pltpu.HBM)


def call(kernel, ins, outs, flops, nbytes, scratch=(), limit=VMEM_LIMIT):
    arrays, specs, buffers = [], [], []
    for x, way in ins:
        if way in ("copy", "scalars", "stay"):
            x = pltpu.with_memory_space_constraint(x, pltpu.HBM)
        if way == "copy":
            buffers.append(pltpu.VMEM(x.shape, x.dtype))
        if way == "scalars":
            buffers.append(pltpu.SMEM(x.shape, x.dtype))
        arrays.append(x)
        specs.append({"smem": SMEM, "vmem": VMEM}.get(way, HBM))
    ways = [way for _, way in ins]
    copied = [i for i, way in enumerate(ways) if way in ("copy", "scalars")]
    if copied:
        buffers.append(pltpu.SemaphoreType.DMA((len(copied),)))

    def body(*refs):
        refs = list(refs)
        if copied:
            given = refs[len(refs) - len(buffers) : -1]
            sems = refs[-1]
            refs = refs[: len(refs) - len(buffers)]
            copies = [pltpu.make_async_copy(refs[i], given[k], sems.at[k]) for k, i in enumerate(copied)]
            for copy in copies:
                copy.start()
            for copy in copies:
                copy.wait()
            for k, i in enumerate(copied):
                refs[i] = given[k]
        kernel(*refs)

    return pl.pallas_call(
        body,
        out_shape=outs,
        in_specs=specs,
        out_specs=jax.tree.map(lambda _: VMEM, outs),
        scratch_shapes=list(scratch) + buffers,
        compiler_params=pltpu.CompilerParams(vmem_limit_bytes=limit),
        cost_estimate=pl.CostEstimate(flops=flops, bytes_accessed=nbytes, transcendentals=0),
    )(*arrays)


def on_device(
    tokens, expert_ids, bucket_codes, route_weights, cotangent, counts, comp_scale, w_gate, w_up, w_down
):
    tok_count, width = tokens.shape
    n = lax.axis_size("expert")
    parts = lax.axis_size("dp")
    local, _, ff = w_gate.shape
    expert_total = counts.shape[0]
    half = width // HALVES
    rows = n * PAIR_ROWS
    total = n * BLOCK_ROWS
    most = n * MOST
    group = lax.axis_index("expert").astype(jnp.int32).reshape(1)
    dp = lax.axis_index("dp").astype(jnp.int32).reshape(1)
    ids, codes, weights = expert_ids.T, bucket_codes.T, route_weights.T
    block_bytes = total * width
    picks = ids.shape[0]

    def layout(way):
        if way == "permute":
            return [jax.ShapeDtypeStruct((BLOCK_ROWS, half), BF16)] * n
        return [jax.ShapeDtypeStruct((n, BLOCK_ROWS, half), BF16)]

    def exchange(way, values):
        if way == "permute":
            return [values[0]] + [
                lax.ppermute(values[k], "expert", [(i, i ^ k) for i in range(n)])
                for k in sorted(range(1, n))
            ]
        return [lax.all_to_all(values[0], "expert", split_axis=0, concat_axis=0, tiled=True)]

    def exchange_dp(values):
        return [values[0]] + [
            lax.ppermute(values[k], "dp", [(i, i ^ k) for i in range(parts)]) for k in range(1, parts)
        ]

    scalars = (counts, "scalars")
    place = (group, "smem")
    copy = lambda *xs: [(x, "copy") for x in xs]
    vmem = lambda xs: [(x, "vmem") for x in xs]

    def gather(mean, way, x):
        return call(
            functools.partial(gather_kernel, mean, n),
            [place, scalars] + copy(ids, codes, weights, x),
            layout(way),
            2 * total * tok_count * width,
            block_bytes,
        )

    base = jax.ShapeDtypeStruct((tok_count, width), F32)
    mix = jax.ShapeDtypeStruct((HALVES * tok_count, total), BF16)
    sent_c = gather(True, WAY_C, tokens)
    got_c = exchange(WAY_C, sent_c)
    sent_p = gather(False, WAY_P, tie(cotangent, sent_c[0]))
    if TIE_P:
        sent_p = [tie(sent_p[0], [got_c[k] for k in TIE_P])] + list(sent_p[1:])
    got_p = exchange(WAY_P, sent_p)
    base_l, base_g, mix_l, mix_g = call(
        functools.partial(prepare_kernel, n),
        [scalars, place] + copy(ids, codes, weights, tie(tokens, sent_p[0]), cotangent, comp_scale),
        [base, base, mix, mix],
        4 * tok_count * expert_total * width,
        5 * tok_count * width * 4,
    )

    def spread(base, mix, got):
        return call(
            functools.partial(spread_kernel, n),
            [place] + copy(base, mix, *got),
            jax.ShapeDtypeStruct(tokens.shape, BF16),
            2 * total * tok_count * width,
            block_bytes,
        )

    if PREPARE_EARLY:
        got_c, base_l, base_g, mix_l, mix_g = lax.optimization_barrier((got_c, base_l, base_g, mix_l, mix_g))
    weight_bytes = 3 * local * width * ff * 2
    expert_flops = 2 * 3 * rows * local * width * ff
    out_o, out_b = layout(WAY_O), layout(WAY_B)
    stream = [
        pltpu.VMEM(w_gate.shape, BF16),
        pltpu.VMEM(w_up.shape, BF16),
        pltpu.VMEM(w_down.shape, BF16),
        pltpu.SemaphoreType.DMA((local * ff // FF_TILE, 3)),
    ]
    fixed = [scalars, place] + copy(comp_scale) + [(w, "stay") for w in (w_gate, w_up, w_down)]

    results = call(
        functools.partial(forward_kernel, n, len(got_c), len(out_o)),
        fixed + copy(*got_c),
        out_o
        + [
            jax.ShapeDtypeStruct((rows, ff), BF16),
            jax.ShapeDtypeStruct((local, ff, most), F32),
            jax.ShapeDtypeStruct((local, ff, most), F32),
        ],
        expert_flops,
        weight_bytes,
        [pltpu.VMEM((rows, width), BF16), pltpu.VMEM((local, most, width), F32)] + stream,
        EXPERT_LIMIT,
    )
    sent_o, (hidden, slope, silu) = results[: len(out_o)], results[len(out_o) :]
    if TIE_O:
        sent_o = tie(list(sent_o), got_p)
    got_o = exchange(WAY_O, sent_o)
    if GATHER_HIDDEN:
        all_hidden = [lax.all_gather(hidden, "dp")]
    else:
        all_hidden = exchange_dp([hidden] * parts)

    pull_and_shares = call(
        functools.partial(unpack_kernel, n, len(got_p), parts),
        [(dp, "smem"), place] + copy(*got_p),
        [jax.ShapeDtypeStruct((rows, width), BF16)]
        + [jax.ShapeDtypeStruct((rows, width // parts), BF16)] * parts,
        2 * rows * min(n, CHUNK) * BLOCK_ROWS * width,
        2 * block_bytes,
    )
    pull = pull_and_shares[0]
    all_shares = exchange_dp(pull_and_shares[1:])

    sent_b = call(
        functools.partial(backward_kernel, n, len(out_b)),
        fixed + copy(pull, slope, silu),
        out_b,
        expert_flops,
        weight_bytes,
        [pltpu.VMEM((local, width, most), BF16), pltpu.VMEM((local, width, most), F32)] + stream,
        EXPERT_LIMIT,
    )
    if TIE_B == "hidden":
        sent_b = tie(sent_b, all_hidden)
    if TIE_B == "both":
        sent_b = tie(sent_b, (all_hidden, all_shares))
    got_b = exchange(WAY_B, sent_b)

    layer_output = spread(base_l, mix_l, got_o)
    if TIE_L:
        all_shares = tie(all_shares, layer_output)
    grad_down = call(
        functools.partial(grad_kernel, n, parts),
        [scalars, place, (dp, "smem")] + copy(*all_hidden, *all_shares),
        jax.ShapeDtypeStruct((local, ff, width // parts), BF16),
        2 * parts * rows * ff * local * width // parts,
        parts * rows * (ff + width // parts) * 2,
    )
    if TIE_G:
        base_g = tie(base_g, (layer_output, grad_down))
    grad_tokens = spread(base_g, mix_g, got_b)
    return (layer_output, grad_tokens, grad_down)


def tie(x, after):
    return lax.optimization_barrier((x, after))[0]


def solution(mesh):
    token_spec = P(("dp", "expert"), None)
    weight_spec = P("expert", None, None)
    in_specs = (token_spec,) * 5 + (P(), P()) + (weight_spec,) * 3
    out_specs = (token_spec, token_spec, P("expert", None, "dp"))
    return jax.shard_map(
        on_device, mesh=mesh, in_specs=in_specs, out_specs=out_specs, check_vma=False
    )
```

```python
import functools

import jax
import jax.numpy as jnp
from jax import lax
from jax.experimental import pallas as pl
from jax.experimental.pallas import tpu as pltpu
from jax.sharding import PartitionSpec as P

PAIR_ROWS = 20
MOST = 16
HALVES = 2
BLOCK_ROWS = HALVES * PAIR_ROWS
CHUNK = 8
FF_TILE = 256
VMEM_LIMIT = 64 * 1024 * 1024 - 65536
AHEAD = 6
SLOPE = jnp.bfloat16
TURN = 1
JOIN = True
TIE_O = ()
TIE_S = False
TIE_L = True
TIE_P = (4, 5, 6, 7)
NEAR = (1, 2, 3)
TIE_B = "hidden"
TIE_G = True
F32 = jnp.float32
BF16 = jnp.bfloat16

NN = (((1,), (0,)), ((), ()))
NT = (((1,), (1,)), ((), ()))
TN = (((0,), (0,)), ((), ()))


def mm(a, b, dims=NN):
    return lax.dot_general(a, b, dims, preferred_element_type=F32)


def iota(shape, dim):
    return lax.broadcasted_iota(jnp.int32, shape, dim)


def places_of(ids, codes, counts_ref):
    count = jnp.zeros_like(ids)
    base = jnp.zeros_like(ids)
    for expert in range(counts_ref.shape[0]):
        hit = ids == expert
        count = jnp.where(hit, counts_ref[expert], count)
        if expert % 2:
            base = jnp.where(hit, counts_ref[expert - 1], base)
    laps = jnp.floor((codes.astype(F32) + 0.5) / count.astype(F32)).astype(jnp.int32)
    return ids >> 1, base + codes - laps * count


def membership(rows, total, values):
    picks, tokens = rows.shape
    index = iota((total, tokens), 0)
    parts = []
    for half in range(HALVES):
        part = jnp.zeros((total, tokens), F32)
        for pick in range(picks):
            hit = index == rows[pick : pick + 1, :] + half * PAIR_ROWS
            value = 1.0 if values is None else values[pick : pick + 1, :]
            part = jnp.where(hit, value, part)
        parts.append(part)
    return jnp.concatenate(parts, axis=1)


def split_halves(x):
    width = x.shape[1] // HALVES
    return jnp.concatenate([x[:, :width], x[:, width:]], axis=0)


def row_places(row, blocks):
    inside = jnp.floor((row.astype(F32) + 0.5) * (1.0 / blocks)).astype(jnp.int32)
    return (row - inside * blocks) * BLOCK_ROWS + inside


def unpack_rows(blocks):
    flat = jnp.concatenate(blocks, axis=0)
    count = len(blocks)
    shape = (count * PAIR_ROWS, count * BLOCK_ROWS)
    place = row_places(iota(shape, 0), count)
    col = iota(shape, 1)
    out = []
    for half in range(HALVES):
        pick = (col == place + half * PAIR_ROWS).astype(F32).astype(BF16)
        out.append(mm(pick, flat).astype(BF16))
    return jnp.concatenate(out, axis=1)


class Blocks:
    def __init__(self, refs, n, group):
        self.refs, self.n, self.group = refs, n, group

    def at(self, j):
        if len(self.refs) == self.n:
            return self.refs[j]
        if len(self.refs) > 1:
            return self.refs[j // 2].at[(j % 2) ^ (self.group & 1)]
        return self.refs[0].at[self.group ^ j]

    def load(self, start, stop):
        return [self.at(j)[...] for j in range(start, stop)]

    def store(self, start, flat):
        for j in range(flat.shape[0] // BLOCK_ROWS):
            self.at(start + j)[...] = flat[j * BLOCK_ROWS : (j + 1) * BLOCK_ROWS].astype(BF16)


def pack_windows(parts, n, c, size, counts_ref, group, dims):
    total = None
    for e, (x, (start, stop)) in enumerate(zip(parts, windows(n))):
        shape = (size * BLOCK_ROWS, stop - start)
        row = iota(shape, 0)
        index = iota(shape, 1) + start
        inside = jnp.floor((index.astype(F32) + 0.5) * (1.0 / n)).astype(jnp.int32)
        place = (index - inside * n - c) * BLOCK_ROWS + inside
        first = inside < counts_ref[2 * group]
        place = jnp.where(first if e == 0 else jnp.logical_not(first), place, -BLOCK_ROWS * n)
        if n > size:
            block = index - inside * n
            place = jnp.where((block >= c) & (block < c + size), place, -BLOCK_ROWS * n)
        picks = [(row == place + h * PAIR_ROWS).astype(F32).astype(BF16) for h in range(HALVES)]
        part = None
        half = x.shape[1 if dims == NN else 0] // HALVES
        for h, pick in enumerate(picks):
            piece = x[:, h * half : (h + 1) * half] if dims == NN else x[h * half : (h + 1) * half, :]
            product = mm(pick, piece, dims)
            part = product if part is None else part + product
        total = part if total is None else total + part
    return total


def windows(n):
    return (0, MOST * n), ((PAIR_ROWS - MOST) * n, PAIR_ROWS * n)


def owned(e, start, stop, n, counts_ref, group):
    index = iota((stop - start, 1), 0) + start
    first = index < counts_ref[2 * group] * n
    return first if e == 0 else jnp.logical_not(first)


def gather_kernel(mean, n, group_ref, counts_ref, ids_ref, codes_ref, weights_ref, x_ref, *outs):
    group = group_ref[0]
    device, inside = places_of(ids_ref[...], codes_ref[...], counts_ref)
    rows = (device ^ group) * BLOCK_ROWS + inside
    member = membership(rows, n * BLOCK_ROWS, None if mean else weights_ref[...])
    sums = mm(member.astype(BF16), split_halves(x_ref[...]))
    if mean:
        sums = sums / jnp.maximum(jnp.sum(member, axis=1, keepdims=True), 1.0)
    Blocks(outs, n, group).store(0, sums)


def gather_pair_kernel(mean, n, group_ref, counts_ref, *refs):
    sources, outs = (refs[:4], refs[4:8]), refs[8:]
    group = group_ref[0]
    core = group & 1
    for mate, (ids_ref, codes_ref, weights_ref, x_ref) in enumerate(sources):
        rows = pair_rows(ids_ref, codes_ref, counts_ref, group)
        member = membership(rows, len(outs) * BLOCK_ROWS, None if mean else weights_ref[...])
        sums = mm(member.astype(BF16), split_halves(x_ref[...]))
        if mean:
            sums = sums / jnp.maximum(jnp.sum(member, axis=1, keepdims=True), 1.0)
        for d, out in enumerate(outs):
            out[core ^ mate] = sums[d * BLOCK_ROWS : (d + 1) * BLOCK_ROWS].astype(BF16)


def own_scale(scale_ref, group, e):
    row = iota(scale_ref.shape, 0)
    return jnp.sum(jnp.where(row == 2 * group + e, scale_ref[...].astype(F32), 0.0), axis=0, keepdims=True)


def gain_of(ids, weights, scale):
    experts, tokens = scale.shape[0], ids.shape[1]
    expert = iota((experts, tokens), 0)
    mix = jnp.zeros((experts, tokens), F32)
    for pick in range(ids.shape[0]):
        mix = jnp.where(expert == ids[pick : pick + 1, :], weights[pick : pick + 1, :], mix)
    high = mix.astype(BF16)
    low = (mix - high.astype(F32)).astype(BF16)
    return mm(high, scale, TN) + mm(low, scale, TN)


def pair_rows(ids_ref, codes_ref, counts_ref, group):
    device, inside = places_of(ids_ref[...], codes_ref[...], counts_ref)
    away = (device >> 1) ^ (group >> 1)
    return jnp.where((device & 1) == (group & 1), away * BLOCK_ROWS + inside, -BLOCK_ROWS)


def prepare_kernel(n, counts_ref, group_ref, ids_ref, codes_ref, weights_ref, *refs):
    mate, (mix_g_ref, mix_own_ref, mix_mate_ref) = refs[:-3], refs[-3:]
    device, inside = places_of(ids_ref[...], codes_ref[...], counts_ref)
    rows = (device ^ group_ref[0]) * BLOCK_ROWS + inside
    member = membership(rows, n * BLOCK_ROWS, None)
    divisor = jnp.maximum(jnp.sum(member, axis=1, keepdims=True), 1.0)
    mix_g_ref[...] = (member / divisor).T.astype(BF16)
    for out, (i, c, w) in ((mix_own_ref, (ids_ref, codes_ref, weights_ref)), (mix_mate_ref, mate)):
        rows = pair_rows(i, c, counts_ref, group_ref[0])
        out[...] = membership(rows, n // 2 * BLOCK_ROWS, w[...]).T.astype(BF16)


def part_kernel(group_ref, mix_ref, *refs):
    blocks, out_ref = refs[:-1], refs[-1]
    flat = jnp.concatenate([b[(group_ref[0] & 1) ^ 1] for b in blocks], axis=0)
    back = mm(mix_ref[...], flat)
    tokens, width = out_ref.shape
    half = width // HALVES
    for h in range(HALVES):
        out_ref[:, h * half : (h + 1) * half] = back[h * tokens : (h + 1) * tokens].astype(BF16)


def spread_kernel(copies, n, pair, group_ref, ids_ref, weights_ref, scale_ref, x_ref, mix_ref, *refs):
    out_hbm, out_ref, sem = refs[-3:]
    given = refs[:-3]
    waits = iter(sorted(copies))
    take = lambda count: [copies[next(waits)].wait() for _ in range(count)]
    group = group_ref[0]
    take(3)
    gain = gain_of(ids_ref[...], weights_ref[...], scale_ref[...])
    take(1)
    base = gain * x_ref[...].astype(F32)
    take(1 + len(given))
    if pair:
        part_ref, blocks = given[0], given[1:]
        base = base + part_ref[...].astype(F32)
        flat = jnp.concatenate([b[group & 1] for b in blocks], axis=0)
    else:
        flat = jnp.concatenate(Blocks(given, n, group).load(0, n), axis=0)
    tokens, width = out_ref.shape
    half = width // HALVES
    sends = []
    for h in range(HALVES):
        cols = pl.ds(h * half, half)
        back = mm(mix_ref[h * tokens : (h + 1) * tokens, :], flat)
        out_ref[:, h * half : (h + 1) * half] = (base[:, h * half : (h + 1) * half] + back).astype(BF16)
        sends.append(pltpu.make_async_copy(out_ref.at[:, cols], out_hbm.at[:, cols], sem.at[h]))
        sends[-1].start()
    for send in sends:
        send.wait()


class Weights:
    def __init__(self, hbm, vmem, sems):
        self.hbm, self.vmem, self.sems = hbm, vmem, sems
        self.per = vmem[0].shape[2] // FF_TILE
        self.steps = vmem[0].shape[0] * self.per

    def views(self, s):
        e = s // self.per
        cols = pl.ds(pl.multiple_of((s - e * self.per) * FF_TILE, FF_TILE), FF_TILE)
        return [(e, slice(None), cols)] * 2 + [(e, cols, slice(None))]

    def copies(self, s):
        return [
            pltpu.make_async_copy(h.at[view], v.at[view], self.sems.at[s, i])
            for i, (h, v, view) in enumerate(zip(self.hbm, self.vmem, self.views(s)))
        ]

    def start(self, s):
        for copy in self.copies(s):
            copy.start()

    def run(self, body):
        for e in range(self.vmem[0].shape[0]):

            def step(f, carry):
                s = e * self.per + f

                @pl.when(s + AHEAD < self.steps)
                def _():
                    self.start(s + AHEAD)

                for copy in self.copies(s):
                    copy.wait()
                cols = pl.ds(pl.multiple_of(f * FF_TILE, FF_TILE), FF_TILE)
                body(e, cols, *[v.at[view] for v, view in zip(self.vmem, self.views(s))])
                return carry

            lax.fori_loop(0, self.per, step, 0)


def unpack_all(x_ref, blocks, n):
    size = min(CHUNK, n)
    for c in range(0, n, size):
        part = unpack_rows(blocks.load(c, c + size))
        if n == size:
            x_ref[...] = part
        else:
            for r in range(PAIR_ROWS):
                x_ref[r * n + c : r * n + c + size, :] = part[r * size : (r + 1) * size]


def forward_kernel(n, n_in, n_out, counts_ref, group_ref, scale_ref, wg_hbm, wu_hbm, wd_hbm, *refs):
    group = group_ref[0]
    blocks, outs = Blocks(refs[:n_in], n, group), Blocks(refs[n_in : n_in + n_out], n, group)
    hidden_ref, slope_ref, silu_ref, x_ref, acc_ref, wg_ref, wu_ref, wd_ref, sems = refs[n_in + n_out :]
    weights = Weights((wg_hbm, wu_hbm, wd_hbm), (wg_ref, wu_ref, wd_ref), sems)
    for s in range(AHEAD):
        weights.start(s)
    unpack_all(x_ref, blocks, n)
    hidden_ref[...] = jnp.zeros_like(hidden_ref)
    for e, (start, stop) in enumerate(windows(n)):
        scale = own_scale(scale_ref, group, e)
        acc_ref[e] = -(scale * x_ref[start:stop, :].astype(F32))

    def body(e, cols, wg, wu, wd):
        start, stop = windows(n)[e]
        mine = owned(e, start, stop, n, counts_ref, group)
        x = x_ref[start:stop, :]
        gate = mm(x, wg[...])
        up = mm(x, wu[...])
        sg = 1.0 / (1.0 + jnp.exp(-gate))
        silu = gate * sg
        hidden = (silu * up).astype(BF16)
        slope = up * sg * (1.0 + gate * (1.0 - sg))
        acc_ref[e] += mm(hidden, wd[...])
        hidden_ref[start:stop, cols] = jnp.where(mine, hidden, hidden_ref[start:stop, cols])
        slope_ref[e, cols, :] = slope.T.astype(SLOPE)
        silu_ref[e, cols, :] = silu.T.astype(SLOPE)

    weights.run(body)
    size = min(n, CHUNK)
    parts = [acc_ref[e].astype(BF16) for e in range(2)]
    for c in range(0, n, size):
        outs.store(c, pack_windows(parts, n, c, size, counts_ref, group, NN))


def backward_kernel(n, n_in, n_out, parts, counts_ref, group_ref, dp_ref, scale_ref, wg_hbm, wu_hbm, wd_hbm, slope_ref, silu_ref, *refs):
    group = group_ref[0]
    blocks, outs = Blocks(refs[:n_in], n, group), Blocks(refs[n_in : n_in + n_out], n, group)
    refs = refs[n_in + n_out :]
    shares, (pull_ref, turned_ref, acc_ref, wg_ref, wu_ref, wd_ref, sems) = refs[:parts], refs[parts:]
    weights = Weights((wg_hbm, wu_hbm, wd_hbm), (wg_ref, wu_ref, wd_ref), sems)
    for s in range(AHEAD):
        weights.start(s)
    unpack_all(pull_ref, blocks, n)
    for e, (start, stop) in enumerate(windows(n)):
        if TURN == 1:
            turned_ref[e] = pull_ref[start:stop, :].T
            scale = jnp.broadcast_to(own_scale(scale_ref, group, e), (8, pull_ref.shape[1])).T[:, :1]
            acc_ref[e] = -(scale * turned_ref[e].astype(F32))
        else:
            pull = pull_ref[start:stop, :].astype(F32)
            turned_ref[e] = pull.T.astype(BF16)
            acc_ref[e] = -(own_scale(scale_ref, group, e) * pull).T
    width = pull_ref.shape[1] // parts
    for k, share in enumerate(shares):
        start = pl.multiple_of((dp_ref[0] ^ k) * width, width)
        share[...] = pull_ref[:, pl.ds(start, width)]

    def body(e, cols, wg, wu, wd):
        d_hidden = mm(wd[...], turned_ref[e])
        d_gate = (d_hidden * slope_ref[e, cols, :].astype(F32)).astype(BF16)
        d_up = (d_hidden * silu_ref[e, cols, :].astype(F32)).astype(BF16)
        if JOIN:
            both = jnp.concatenate([wg[...], wu[...]], axis=1)
            acc_ref[e] += mm(both, jnp.concatenate([d_gate, d_up], axis=0))
        else:
            acc_ref[e] += mm(wg[...], d_gate) + mm(wu[...], d_up)

    weights.run(body)
    size = min(n, CHUNK)
    sums = [acc_ref[e].astype(BF16) for e in range(2)]
    for c in range(0, n, size):
        outs.store(c, pack_windows(sums, n, c, size, counts_ref, group, NT))


def grad_kernel(n, parts, counts_ref, group_ref, *refs):
    hidden, shares = refs[:parts], refs[parts : 2 * parts]
    out_hbm, out_ref, sem = refs[2 * parts :]
    sends = []
    for e in range(2):
        start, stop = windows(n)[e]
        mine = owned(e, start, stop, n, counts_ref, group_ref[0])
        h_all = jnp.concatenate([h[start:stop, :] for h in hidden], axis=0)
        pull = jnp.concatenate(
            [jnp.where(mine, s[start:stop, :].astype(F32), 0.0).astype(BF16) for s in shares], axis=0
        )
        out_ref[e] = mm(h_all, pull, TN).astype(BF16)
        sends.append(pltpu.make_async_copy(out_ref.at[e], out_hbm.at[e], sem.at[e]))
        sends[-1].start()
    for send in sends:
        send.wait()


SMEM = pl.BlockSpec(memory_space=pltpu.SMEM)
VMEM = pl.BlockSpec(memory_space=pltpu.VMEM)
HBM = pl.BlockSpec(memory_space=pltpu.HBM)


def call(kernel, ins, outs, flops, nbytes, scratch=(), lazy=False, out_spec=VMEM):
    arrays, specs, buffers = [], [], []
    for x, way in ins:
        if way in ("copy", "scalars", "stay"):
            x = pltpu.with_memory_space_constraint(x, pltpu.HBM)
        if way == "copy":
            buffers.append(pltpu.VMEM(x.shape, x.dtype))
        if way == "scalars":
            buffers.append(pltpu.SMEM(x.shape, x.dtype))
        arrays.append(x)
        specs.append(SMEM if way == "smem" else HBM)
    copied = [i for i, (_, way) in enumerate(ins) if way in ("copy", "scalars")]
    buffers.append(pltpu.SemaphoreType.DMA((max(len(copied), 1),)))

    def body(*refs):
        refs = list(refs)
        given, sems = refs[len(refs) - len(buffers) : -1], refs[-1]
        refs = refs[: len(refs) - len(buffers)]
        copies = {i: pltpu.make_async_copy(refs[i], given[k], sems.at[k]) for k, i in enumerate(copied)}
        for copy in copies.values():
            copy.start()
        for k, i in enumerate(copied):
            refs[i] = given[k]
        if lazy:
            kernel(copies, *refs)
        else:
            for copy in copies.values():
                copy.wait()
            kernel(*refs)

    return pl.pallas_call(
        body,
        out_shape=outs,
        in_specs=specs,
        out_specs=jax.tree.map(lambda _: out_spec, outs),
        scratch_shapes=list(scratch) + buffers,
        compiler_params=pltpu.CompilerParams(vmem_limit_bytes=VMEM_LIMIT),
        cost_estimate=pl.CostEstimate(flops=flops, bytes_accessed=nbytes, transcendentals=0),
    )(*arrays)


def on_device(
    tokens, expert_ids, bucket_codes, route_weights, cotangent, counts, comp_scale, w_gate, w_up, w_down
):
    tok_count, width = tokens.shape
    n = lax.axis_size("expert")
    parts = lax.axis_size("dp")
    local, _, ff = w_gate.shape
    expert_total = counts.shape[0]
    half = width // HALVES
    rows = n * PAIR_ROWS
    total = n * BLOCK_ROWS
    most = n * MOST
    group = lax.axis_index("expert").astype(jnp.int32).reshape(1)
    dp = lax.axis_index("dp").astype(jnp.int32).reshape(1)
    ids, codes, weights = expert_ids.T, bucket_codes.T, route_weights.T
    block_bytes = total * width
    picks = ids.shape[0]

    block = (BLOCK_ROWS, half)

    def layout(way):
        if way == "permute":
            return [jax.ShapeDtypeStruct(block, BF16)] * n
        if way == "pair":
            return [jax.ShapeDtypeStruct((2, *block), BF16)] * (n // 2)
        return [jax.ShapeDtypeStruct((n, *block), BF16)]

    def exchange(way, values):
        if way == "all":
            return [lax.all_to_all(values[0], "expert", split_axis=0, concat_axis=0, tiled=True)]
        step = n // len(values)
        return [values[0]] + [
            lax.ppermute(values[d], "expert", [(i, i ^ (step * d)) for i in range(n)])
            for d in range(1, len(values))
        ]

    def from_mate(x):
        return lax.ppermute(x, "expert", [(i, i ^ 1) for i in range(n)])

    def exchange_dp(values):
        return [values[0]] + [
            lax.ppermute(values[k], "dp", [(i, i ^ k) for i in range(parts)]) for k in range(1, parts)
        ]

    scalars = (counts, "scalars")
    place = (group, "smem")
    copy = lambda *xs: [(x, "copy") for x in xs]
    vmem = lambda xs: [(x, "vmem") for x in xs]

    mate = [from_mate(v).T for v in (expert_ids, bucket_codes, route_weights)]

    def gather(mean, way, x):
        kernel, given = gather_kernel, [ids, codes, weights, x]
        if way == "pair":
            kernel, given = gather_pair_kernel, given + mate + [from_mate(x)]
        return call(
            functools.partial(kernel, mean, n),
            [place, scalars] + copy(*given),
            layout(way),
            2 * total * tok_count * width,
            block_bytes,
        )

    sent_c = list(gather(True, "permute", tokens))
    sent_p = list(gather(False, "pair", tie(cotangent, sent_c[0])))
    if NEAR:
        near = [sent_c[k] for k in NEAR]
        for k, v in zip(NEAR, tie(near, sent_p)):
            sent_c[k] = v
    got_c = exchange("permute", sent_c)
    if TIE_P:
        sent_p = tie(sent_p, [got_c[k] for k in TIE_P])
    got_p = exchange("pair", sent_p)

    weight_bytes = 3 * local * width * ff * 2
    expert_flops = 2 * 3 * rows * local * width * ff
    out_o, out_b = layout("pair"), layout("all")
    stream = [
        pltpu.VMEM(w_gate.shape, BF16),
        pltpu.VMEM(w_up.shape, BF16),
        pltpu.VMEM(w_down.shape, BF16),
        pltpu.SemaphoreType.DMA((local * ff // FF_TILE, 3)),
    ]
    fixed = [scalars, place] + copy(comp_scale) + [(w, "stay") for w in (w_gate, w_up, w_down)]

    results = call(
        functools.partial(forward_kernel, n, len(got_c), len(out_o)),
        fixed + copy(*got_c),
        out_o
        + [
            jax.ShapeDtypeStruct((rows, ff), BF16),
            jax.ShapeDtypeStruct((local, ff, most), SLOPE),
            jax.ShapeDtypeStruct((local, ff, most), SLOPE),
        ],
        expert_flops,
        weight_bytes,
        [pltpu.VMEM((rows, width), BF16), pltpu.VMEM((local, most, width), F32)] + stream,
    )
    mix = jax.ShapeDtypeStruct((HALVES * tok_count, total), BF16)
    mix_pair = jax.ShapeDtypeStruct((HALVES * tok_count, total // 2), BF16)
    mix_g, mix_own, mix_mate = call(
        functools.partial(prepare_kernel, n),
        [scalars, place] + copy(tie(ids, results[0]), codes, weights, *mate),
        [mix, mix_pair, mix_pair],
        0,
        3 * tok_count * total * 4,
    )
    sent_o, (hidden, slope, silu) = results[: len(out_o)], results[len(out_o) :]
    if TIE_O:
        sent_o = tie(list(sent_o), [got_p[d] for d in TIE_O])
    got_o = exchange("pair", sent_o)
    all_hidden = exchange_dp([hidden] * parts)

    share = jax.ShapeDtypeStruct((rows, width // parts), BF16)
    results = call(
        functools.partial(backward_kernel, n, len(got_p), len(out_b), parts),
        fixed[:2] + [(dp, "smem")] + fixed[2:] + copy(slope, silu, *got_p),
        out_b + [share] * parts,
        expert_flops,
        weight_bytes,
        [
            pltpu.VMEM((rows, width), BF16),
            pltpu.VMEM((local, width, most), BF16),
            pltpu.VMEM((local, width, most), F32),
        ]
        + stream,
    )
    sent_b, shares = results[: len(out_b)], results[len(out_b) :]
    all_shares = exchange_dp(shares)
    if TIE_B == "hidden":
        sent_b = tie(list(sent_b), (all_hidden, got_o))
    if TIE_B == "both":
        sent_b = tie(sent_b, (all_hidden, all_shares))
    got_b = exchange("all", sent_b)

    part = call(
        part_kernel,
        [place] + copy(mix_mate, *got_o),
        jax.ShapeDtypeStruct(tokens.shape, BF16),
        total * tok_count * width,
        block_bytes,
    )

    def spread(pair, x, mix, given):
        out = jax.ShapeDtypeStruct(tokens.shape, BF16)
        return call(
            lambda copies, *refs: spread_kernel(copies, n, pair, *refs),
            [place] + copy(ids, weights, comp_scale, x, mix, *given),
            out,
            2 * total * tok_count * width,
            block_bytes,
            [pltpu.VMEM(out.shape, BF16), pltpu.SemaphoreType.DMA((HALVES,))],
            lazy=True,
            out_spec=HBM,
        )

    if TIE_S:
        mix_own = tie(mix_own, all_shares)
    layer_output = spread(True, tokens, mix_own, [from_mate(part), *got_o])
    if TIE_L:
        all_shares = tie(all_shares, layer_output)
    grad_shape = jax.ShapeDtypeStruct((local, ff, width // parts), BF16)
    grad_down = call(
        functools.partial(grad_kernel, n, parts),
        [scalars, place] + copy(*all_hidden, *all_shares),
        grad_shape,
        2 * parts * rows * ff * local * width // parts,
        parts * rows * (ff + width // parts) * 2,
        [pltpu.VMEM(grad_shape.shape, BF16), pltpu.SemaphoreType.DMA((local,))],
        out_spec=HBM,
    )
    if TIE_G:
        mix_g = tie(mix_g, (layer_output, grad_down))
    grad_tokens = spread(False, cotangent, mix_g, got_b)
    return (layer_output, grad_tokens, grad_down)


def tie(x, after):
    return lax.optimization_barrier((x, after))[0]


def solution(mesh):
    token_spec = P(("dp", "expert"), None)
    weight_spec = P("expert", None, None)
    in_specs = (token_spec,) * 5 + (P(), P()) + (weight_spec,) * 3
    out_specs = (token_spec, token_spec, P("expert", None, "dp"))
    return jax.shard_map(
        on_device, mesh=mesh, in_specs=in_specs, out_specs=out_specs, check_vma=False
    )
```

```python
import functools

import jax
import jax.numpy as jnp
from jax import lax
from jax.experimental import pallas as pl
from jax.experimental.pallas import tpu as pltpu
from jax.sharding import PartitionSpec as P

PAIR_ROWS = 20
MOST = 16
HALVES = 2
BLOCK_ROWS = HALVES * PAIR_ROWS
CHUNK = 8
FF_TILE = 256
VMEM_LIMIT = 64 * 1024 * 1024 - 65536
AHEAD = 6
SLOPE = jnp.bfloat16
TURN = 1
JOIN = True
TIE_O = ()
TIE_S = True
TIE_L = True
TIE_P = (4,5)
NEAR = (1,)
ORDER_C = ()
MATE_FIRST = ()
CHEAP = 1000000
FIRST_P = False
TIE_B = "hidden"
TIE_G = True
F32 = jnp.float32
BF16 = jnp.bfloat16

NN = (((1,), (0,)), ((), ()))
NT = (((1,), (1,)), ((), ()))
TN = (((0,), (0,)), ((), ()))


def mm(a, b, dims=NN):
    return lax.dot_general(a, b, dims, preferred_element_type=F32)


def iota(shape, dim):
    return lax.broadcasted_iota(jnp.int32, shape, dim)


def places_of(ids, codes, counts_ref):
    count = jnp.zeros_like(ids)
    base = jnp.zeros_like(ids)
    for expert in range(counts_ref.shape[0]):
        hit = ids == expert
        count = jnp.where(hit, counts_ref[expert], count)
        if expert % 2:
            base = jnp.where(hit, counts_ref[expert - 1], base)
    laps = jnp.floor((codes.astype(F32) + 0.5) / count.astype(F32)).astype(jnp.int32)
    return ids >> 1, base + codes - laps * count


def membership(rows, total, values):
    picks, tokens = rows.shape
    index = iota((total, tokens), 0)
    parts = []
    for half in range(HALVES):
        part = jnp.zeros((total, tokens), F32)
        for pick in range(picks):
            hit = index == rows[pick : pick + 1, :] + half * PAIR_ROWS
            value = 1.0 if values is None else values[pick : pick + 1, :]
            part = jnp.where(hit, value, part)
        parts.append(part)
    return jnp.concatenate(parts, axis=1)


def split_halves(x):
    width = x.shape[1] // HALVES
    return jnp.concatenate([x[:, :width], x[:, width:]], axis=0)


def row_places(row, blocks):
    inside = jnp.floor((row.astype(F32) + 0.5) * (1.0 / blocks)).astype(jnp.int32)
    return (row - inside * blocks) * BLOCK_ROWS + inside


def unpack_rows(blocks):
    flat = jnp.concatenate(blocks, axis=0)
    count = len(blocks)
    rows = count * PAIR_ROWS
    shape = (rows, count * BLOCK_ROWS)
    place = row_places(iota(shape, 0), count)
    col = iota(shape, 1)
    picks = [(col == place + half * PAIR_ROWS).astype(F32) for half in range(HALVES)]
    out = mm(jnp.concatenate(picks, axis=0).astype(BF16), flat).astype(BF16)
    return jnp.concatenate([out[h * rows : (h + 1) * rows] for h in range(HALVES)], axis=1)


class Blocks:
    def __init__(self, refs, n, group):
        self.refs, self.n, self.group = refs, n, group

    def at(self, j):
        if len(self.refs) == self.n:
            return self.refs[j]
        if len(self.refs) > 1:
            return self.refs[j // 2].at[(j % 2) ^ (self.group & 1)]
        return self.refs[0].at[self.group ^ j]

    def load(self, start, stop):
        return [self.at(j)[...] for j in range(start, stop)]

    def store(self, start, flat):
        for j in range(flat.shape[0] // BLOCK_ROWS):
            self.at(start + j)[...] = flat[j * BLOCK_ROWS : (j + 1) * BLOCK_ROWS].astype(BF16)


def pack_windows(parts, n, c, size, counts_ref, group, dims):
    picks, pieces = [], []
    half = parts[0].shape[1 if dims == NN else 0] // HALVES
    for e, (x, (start, stop)) in enumerate(zip(parts, windows(n))):
        shape = (size * BLOCK_ROWS, stop - start)
        row = iota(shape, 0)
        index = iota(shape, 1) + start
        inside = jnp.floor((index.astype(F32) + 0.5) * (1.0 / n)).astype(jnp.int32)
        place = (index - inside * n - c) * BLOCK_ROWS + inside
        first = inside < counts_ref[2 * group]
        place = jnp.where(first if e == 0 else jnp.logical_not(first), place, -BLOCK_ROWS * n)
        if n > size:
            block = index - inside * n
            place = jnp.where((block >= c) & (block < c + size), place, -BLOCK_ROWS * n)
        for h in range(HALVES):
            picks.append((row == place + h * PAIR_ROWS).astype(F32).astype(BF16))
            span = slice(h * half, (h + 1) * half)
            pieces.append(x[:, span] if dims == NN else x[span, :])
    return mm(jnp.concatenate(picks, axis=1), jnp.concatenate(pieces, axis=0 if dims == NN else 1), dims)


def windows(n):
    return (0, MOST * n), ((PAIR_ROWS - MOST) * n, PAIR_ROWS * n)


def owned(e, start, stop, n, counts_ref, group):
    index = iota((stop - start, 1), 0) + start
    first = index < counts_ref[2 * group] * n
    return first if e == 0 else jnp.logical_not(first)


def gather_kernel(mean, n, group_ref, counts_ref, ids_ref, codes_ref, weights_ref, x_ref, *outs):
    group = group_ref[0]
    device, inside = places_of(ids_ref[...], codes_ref[...], counts_ref)
    rows = (device ^ group) * BLOCK_ROWS + inside
    member = membership(rows, n * BLOCK_ROWS, None if mean else weights_ref[...])
    sums = mm(member.astype(BF16), split_halves(x_ref[...]))
    if mean:
        sums = sums / jnp.maximum(jnp.sum(member, axis=1, keepdims=True), 1.0)
    Blocks(outs, n, group).store(0, sums)


def gather_pair_kernel(mean, n, group_ref, counts_ref, *refs):
    sources, outs = (refs[:4], refs[4:8]), refs[8:]
    group = group_ref[0]
    core = group & 1
    for mate, (ids_ref, codes_ref, weights_ref, x_ref) in enumerate(sources):
        rows = pair_rows(ids_ref, codes_ref, counts_ref, group)
        member = membership(rows, len(outs) * BLOCK_ROWS, None if mean else weights_ref[...])
        sums = mm(member.astype(BF16), split_halves(x_ref[...]))
        if mean:
            sums = sums / jnp.maximum(jnp.sum(member, axis=1, keepdims=True), 1.0)
        for d, out in enumerate(outs):
            out[core ^ mate] = sums[d * BLOCK_ROWS : (d + 1) * BLOCK_ROWS].astype(BF16)


def own_scale(scale_ref, group, e):
    row = iota(scale_ref.shape, 0)
    return jnp.sum(jnp.where(row == 2 * group + e, scale_ref[...].astype(F32), 0.0), axis=0, keepdims=True)


def gain_of(ids, weights, scale):
    experts, tokens = scale.shape[0], ids.shape[1]
    expert = iota((experts, tokens), 0)
    mix = jnp.zeros((experts, tokens), F32)
    for pick in range(ids.shape[0]):
        mix = jnp.where(expert == ids[pick : pick + 1, :], weights[pick : pick + 1, :], mix)
    high = mix.astype(BF16)
    low = (mix - high.astype(F32)).astype(BF16)
    return mm(high, scale, TN) + mm(low, scale, TN)


def pair_rows(ids_ref, codes_ref, counts_ref, group):
    device, inside = places_of(ids_ref[...], codes_ref[...], counts_ref)
    away = (device >> 1) ^ (group >> 1)
    return jnp.where((device & 1) == (group & 1), away * BLOCK_ROWS + inside, -BLOCK_ROWS)


def prepare_kernel(n, counts_ref, group_ref, ids_ref, codes_ref, weights_ref, *refs):
    mate, (mix_g_ref, mix_own_ref, mix_mate_ref) = refs[:-3], refs[-3:]
    device, inside = places_of(ids_ref[...], codes_ref[...], counts_ref)
    rows = (device ^ group_ref[0]) * BLOCK_ROWS + inside
    member = membership(rows, n * BLOCK_ROWS, None)
    divisor = jnp.maximum(jnp.sum(member, axis=1, keepdims=True), 1.0)
    mix_g_ref[...] = (member / divisor).T.astype(BF16)
    for out, (i, c, w) in ((mix_own_ref, (ids_ref, codes_ref, weights_ref)), (mix_mate_ref, mate)):
        rows = pair_rows(i, c, counts_ref, group_ref[0])
        out[...] = membership(rows, n // 2 * BLOCK_ROWS, w[...]).T.astype(BF16)


def part_kernel(group_ref, mix_ref, *refs):
    blocks, out_ref = refs[:-1], refs[-1]
    flat = jnp.concatenate([b[(group_ref[0] & 1) ^ 1] for b in blocks], axis=0)
    back = mm(mix_ref[...], flat)
    tokens, width = out_ref.shape
    half = width // HALVES
    for h in range(HALVES):
        out_ref[:, h * half : (h + 1) * half] = back[h * tokens : (h + 1) * tokens].astype(BF16)


def spread_kernel(copies, n, pair, group_ref, ids_ref, weights_ref, scale_ref, x_ref, mix_ref, *refs):
    out_hbm, out_ref, sem = refs[-3:]
    given = refs[:-3]
    waits = iter(sorted(copies))
    take = lambda count: [copies[next(waits)].wait() for _ in range(count)]
    group = group_ref[0]
    take(3)
    gain = gain_of(ids_ref[...], weights_ref[...], scale_ref[...])
    take(1)
    base = gain * x_ref[...].astype(F32)
    take(1 + len(given))
    if pair:
        part_ref, blocks = given[0], given[1:]
        base = base + part_ref[...].astype(F32)
        flat = jnp.concatenate([b[group & 1] for b in blocks], axis=0)
    else:
        flat = jnp.concatenate(Blocks(given, n, group).load(0, n), axis=0)
    tokens, width = out_ref.shape
    half = width // HALVES
    sends = []
    for h in range(HALVES):
        cols = pl.ds(h * half, half)
        back = mm(mix_ref[h * tokens : (h + 1) * tokens, :], flat)
        out_ref[:, h * half : (h + 1) * half] = (base[:, h * half : (h + 1) * half] + back).astype(BF16)
        sends.append(pltpu.make_async_copy(out_ref.at[:, cols], out_hbm.at[:, cols], sem.at[h]))
        sends[-1].start()
    for send in sends:
        send.wait()


class Weights:
    def __init__(self, hbm, vmem, sems):
        self.hbm, self.vmem, self.sems = hbm, vmem, sems
        self.per = vmem[0].shape[2] // FF_TILE
        self.steps = vmem[0].shape[0] * self.per

    def views(self, s):
        e = s // self.per
        cols = pl.ds(pl.multiple_of((s - e * self.per) * FF_TILE, FF_TILE), FF_TILE)
        return [(e, slice(None), cols)] * 2 + [(e, cols, slice(None))]

    def copies(self, s):
        return [
            pltpu.make_async_copy(h.at[view], v.at[view], self.sems.at[s, i])
            for i, (h, v, view) in enumerate(zip(self.hbm, self.vmem, self.views(s)))
        ]

    def start(self, s):
        for copy in self.copies(s):
            copy.start()

    def run(self, body):
        for e in range(self.vmem[0].shape[0]):

            def step(f, carry):
                s = e * self.per + f

                @pl.when(s + AHEAD < self.steps)
                def _():
                    self.start(s + AHEAD)

                for copy in self.copies(s):
                    copy.wait()
                cols = pl.ds(pl.multiple_of(f * FF_TILE, FF_TILE), FF_TILE)
                body(e, cols, *[v.at[view] for v, view in zip(self.vmem, self.views(s))])
                return carry

            lax.fori_loop(0, self.per, step, 0)


def unpack_all(x_ref, blocks, n):
    size = min(CHUNK, n)
    for c in range(0, n, size):
        part = unpack_rows(blocks.load(c, c + size))
        if n == size:
            x_ref[...] = part
        else:
            for r in range(PAIR_ROWS):
                x_ref[r * n + c : r * n + c + size, :] = part[r * size : (r + 1) * size]


def forward_kernel(n, n_in, n_out, counts_ref, group_ref, scale_ref, wg_hbm, wu_hbm, wd_hbm, *refs):
    group = group_ref[0]
    blocks, outs = Blocks(refs[:n_in], n, group), Blocks(refs[n_in : n_in + n_out], n, group)
    hidden_ref, slope_ref, silu_ref, x_ref, acc_ref, wg_ref, wu_ref, wd_ref, sems = refs[n_in + n_out :]
    weights = Weights((wg_hbm, wu_hbm, wd_hbm), (wg_ref, wu_ref, wd_ref), sems)
    for s in range(AHEAD):
        weights.start(s)
    unpack_all(x_ref, blocks, n)
    hidden_ref[...] = jnp.zeros_like(hidden_ref)
    for e, (start, stop) in enumerate(windows(n)):
        scale = own_scale(scale_ref, group, e)
        acc_ref[e] = -(scale * x_ref[start:stop, :].astype(F32))

    def body(e, cols, wg, wu, wd):
        start, stop = windows(n)[e]
        mine = owned(e, start, stop, n, counts_ref, group)
        x = x_ref[start:stop, :]
        gate = mm(x, wg[...])
        up = mm(x, wu[...])
        sg = 1.0 / (1.0 + jnp.exp(-gate))
        silu = gate * sg
        hidden = (silu * up).astype(BF16)
        slope = up * sg * (1.0 + gate * (1.0 - sg))
        acc_ref[e] += mm(hidden, wd[...])
        hidden_ref[start:stop, cols] = jnp.where(mine, hidden, hidden_ref[start:stop, cols])
        slope_ref[e, cols, :] = slope.T.astype(SLOPE)
        silu_ref[e, cols, :] = silu.T.astype(SLOPE)

    weights.run(body)
    size = min(n, CHUNK)
    parts = [acc_ref[e].astype(BF16) for e in range(2)]
    for c in range(0, n, size):
        outs.store(c, pack_windows(parts, n, c, size, counts_ref, group, NN))


def backward_kernel(n, n_in, n_out, parts, counts_ref, group_ref, dp_ref, scale_ref, wg_hbm, wu_hbm, wd_hbm, slope_ref, silu_ref, *refs):
    group = group_ref[0]
    blocks, outs = Blocks(refs[:n_in], n, group), Blocks(refs[n_in : n_in + n_out], n, group)
    refs = refs[n_in + n_out :]
    shares, (pull_ref, turned_ref, acc_ref, wg_ref, wu_ref, wd_ref, sems) = refs[:parts], refs[parts:]
    weights = Weights((wg_hbm, wu_hbm, wd_hbm), (wg_ref, wu_ref, wd_ref), sems)
    for s in range(AHEAD):
        weights.start(s)
    unpack_all(pull_ref, blocks, n)
    for e, (start, stop) in enumerate(windows(n)):
        if TURN == 1:
            turned_ref[e] = pull_ref[start:stop, :].T
            scale = jnp.broadcast_to(own_scale(scale_ref, group, e), (8, pull_ref.shape[1])).T[:, :1]
            acc_ref[e] = -(scale * turned_ref[e].astype(F32))
        else:
            pull = pull_ref[start:stop, :].astype(F32)
            turned_ref[e] = pull.T.astype(BF16)
            acc_ref[e] = -(own_scale(scale_ref, group, e) * pull).T
    width = pull_ref.shape[1] // parts
    for k, share in enumerate(shares):
        start = pl.multiple_of((dp_ref[0] ^ k) * width, width)
        share[...] = pull_ref[:, pl.ds(start, width)]

    def body(e, cols, wg, wu, wd):
        d_hidden = mm(wd[...], turned_ref[e])
        d_gate = (d_hidden * slope_ref[e, cols, :].astype(F32)).astype(BF16)
        d_up = (d_hidden * silu_ref[e, cols, :].astype(F32)).astype(BF16)
        if JOIN:
            both = jnp.concatenate([wg[...], wu[...]], axis=1)
            acc_ref[e] += mm(both, jnp.concatenate([d_gate, d_up], axis=0))
        else:
            acc_ref[e] += mm(wg[...], d_gate) + mm(wu[...], d_up)

    weights.run(body)
    size = min(n, CHUNK)
    sums = [acc_ref[e].astype(BF16) for e in range(2)]
    for c in range(0, n, size):
        outs.store(c, pack_windows(sums, n, c, size, counts_ref, group, NT))


def grad_kernel(n, parts, counts_ref, group_ref, *refs):
    hidden, shares = refs[:parts], refs[parts : 2 * parts]
    out_hbm, out_ref, sem = refs[2 * parts :]
    sends = []
    for e in range(2):
        start, stop = windows(n)[e]
        mine = owned(e, start, stop, n, counts_ref, group_ref[0])
        h_all = jnp.concatenate([h[start:stop, :] for h in hidden], axis=0)
        pull = jnp.concatenate(
            [jnp.where(mine, s[start:stop, :].astype(F32), 0.0).astype(BF16) for s in shares], axis=0
        )
        out_ref[e] = mm(h_all, pull, TN).astype(BF16)
        sends.append(pltpu.make_async_copy(out_ref.at[e], out_hbm.at[e], sem.at[e]))
        sends[-1].start()
    for send in sends:
        send.wait()


SMEM = pl.BlockSpec(memory_space=pltpu.SMEM)
VMEM = pl.BlockSpec(memory_space=pltpu.VMEM)
HBM = pl.BlockSpec(memory_space=pltpu.HBM)


def call(kernel, ins, outs, flops, nbytes, scratch=(), lazy=False, out_spec=VMEM):
    arrays, specs, buffers = [], [], []
    for x, way in ins:
        if way in ("copy", "scalars", "stay"):
            x = pltpu.with_memory_space_constraint(x, pltpu.HBM)
        if way == "copy":
            buffers.append(pltpu.VMEM(x.shape, x.dtype))
        if way == "scalars":
            buffers.append(pltpu.SMEM(x.shape, x.dtype))
        arrays.append(x)
        specs.append(SMEM if way == "smem" else HBM)
    copied = [i for i, (_, way) in enumerate(ins) if way in ("copy", "scalars")]
    buffers.append(pltpu.SemaphoreType.DMA((max(len(copied), 1),)))

    def body(*refs):
        refs = list(refs)
        given, sems = refs[len(refs) - len(buffers) : -1], refs[-1]
        refs = refs[: len(refs) - len(buffers)]
        copies = {i: pltpu.make_async_copy(refs[i], given[k], sems.at[k]) for k, i in enumerate(copied)}
        for copy in copies.values():
            copy.start()
        for k, i in enumerate(copied):
            refs[i] = given[k]
        if lazy:
            kernel(copies, *refs)
        else:
            for copy in copies.values():
                copy.wait()
            kernel(*refs)

    return pl.pallas_call(
        body,
        out_shape=outs,
        in_specs=specs,
        out_specs=jax.tree.map(lambda _: out_spec, outs),
        scratch_shapes=list(scratch) + buffers,
        compiler_params=pltpu.CompilerParams(vmem_limit_bytes=VMEM_LIMIT),
        cost_estimate=pl.CostEstimate(flops=flops, bytes_accessed=nbytes, transcendentals=0),
    )(*arrays)


def on_device(
    tokens, expert_ids, bucket_codes, route_weights, cotangent, counts, comp_scale, w_gate, w_up, w_down
):
    tok_count, width = tokens.shape
    n = lax.axis_size("expert")
    parts = lax.axis_size("dp")
    local, _, ff = w_gate.shape
    expert_total = counts.shape[0]
    half = width // HALVES
    rows = n * PAIR_ROWS
    total = n * BLOCK_ROWS
    most = n * MOST
    group = lax.axis_index("expert").astype(jnp.int32).reshape(1)
    dp = lax.axis_index("dp").astype(jnp.int32).reshape(1)
    ids, codes, weights = expert_ids.T, bucket_codes.T, route_weights.T
    block_bytes = total * width
    picks = ids.shape[0]

    block = (BLOCK_ROWS, half)

    def layout(way):
        if way == "permute":
            return [jax.ShapeDtypeStruct(block, BF16)] * n
        if way == "pair":
            return [jax.ShapeDtypeStruct((2, *block), BF16)] * (n // 2)
        return [jax.ShapeDtypeStruct((n, *block), BF16)]

    def exchange(way, values):
        if way == "all":
            return [lax.all_to_all(values[0], "expert", split_axis=0, concat_axis=0, tiled=True)]
        step = n // len(values)
        got = {0: values[0]}
        for d in sorted(range(1, len(values)), key=lambda d: (d not in ORDER_C, ORDER_C.index(d) if d in ORDER_C else d)):
            got[d] = lax.ppermute(values[d], "expert", [(i, i ^ (step * d)) for i in range(n)])
        return [got[d] for d in range(len(values))]

    def from_mate(x):
        return lax.ppermute(x, "expert", [(i, i ^ 1) for i in range(n)])

    def exchange_dp(values):
        return [values[0]] + [
            lax.ppermute(values[k], "dp", [(i, i ^ k) for i in range(parts)]) for k in range(1, parts)
        ]

    scalars = (counts, "scalars")
    place = (group, "smem")
    copy = lambda *xs: [(x, "copy") for x in xs]
    vmem = lambda xs: [(x, "vmem") for x in xs]

    mate = [from_mate(v).T for v in (expert_ids, bucket_codes, route_weights)]

    def gather(mean, way, x):
        kernel, given = gather_kernel, [ids, codes, weights, x]
        if way == "pair":
            kernel, given = gather_pair_kernel, given + mate + [from_mate(x)]
        return call(
            functools.partial(kernel, mean, n),
            [place, scalars] + copy(*given),
            layout(way),
            2 * total * tok_count * width,
            block_bytes,
        )

    sent_c = list(gather(True, "permute", tokens))
    sent_p = list(gather(False, "pair", tie(cotangent, sent_c[0])))
    if NEAR:
        near = [sent_c[k] for k in NEAR]
        for k, v in zip(NEAR, tie(near, sent_p)):
            sent_c[k] = v
    if MATE_FIRST:
        for k, v in zip(MATE_FIRST, tie([sent_c[k] for k in MATE_FIRST], mate[0])):
            sent_c[k] = v
    got_c = exchange("permute", sent_c)
    if FIRST_P:
        early = lax.ppermute(sent_p[1], "expert", [(i, i ^ 2) for i in range(n)])
        late = tie(sent_p[2:], ([got_c[k] for k in TIE_P], early))
        got_p = [sent_p[0], early] + [
            lax.ppermute(v, "expert", [(i, i ^ (2 * d)) for i in range(n)]) for d, v in enumerate(late, 2)
        ]
    else:
        sent_p = tie(sent_p, [got_c[k] for k in TIE_P])
        got_p = exchange("pair", sent_p)

    weight_bytes = 3 * local * width * ff * 2
    expert_flops = 2 * 3 * rows * local * width * ff
    out_o, out_b = layout("pair"), layout("all")
    stream = [
        pltpu.VMEM(w_gate.shape, BF16),
        pltpu.VMEM(w_up.shape, BF16),
        pltpu.VMEM(w_down.shape, BF16),
        pltpu.SemaphoreType.DMA((local * ff // FF_TILE, 3)),
    ]
    fixed = [scalars, place] + copy(comp_scale) + [(w, "stay") for w in (w_gate, w_up, w_down)]

    results = call(
        functools.partial(forward_kernel, n, len(got_c), len(out_o)),
        fixed + copy(*got_c),
        out_o
        + [
            jax.ShapeDtypeStruct((rows, ff), BF16),
            jax.ShapeDtypeStruct((local, ff, most), SLOPE),
            jax.ShapeDtypeStruct((local, ff, most), SLOPE),
        ],
        expert_flops,
        weight_bytes,
        [pltpu.VMEM((rows, width), BF16), pltpu.VMEM((local, most, width), F32)] + stream,
    )
    mix = jax.ShapeDtypeStruct((HALVES * tok_count, total), BF16)
    mix_pair = jax.ShapeDtypeStruct((HALVES * tok_count, total // 2), BF16)
    mix_g, mix_own, mix_mate = call(
        functools.partial(prepare_kernel, n),
        [scalars, place] + copy(tie(ids, results[0]), codes, weights, *mate),
        [mix, mix_pair, mix_pair],
        0,
        3 * tok_count * total * 4 // CHEAP,
    )
    sent_o, (hidden, slope, silu) = results[: len(out_o)], results[len(out_o) :]
    if TIE_O:
        sent_o = tie(list(sent_o), [got_p[d] for d in TIE_O])
    got_o = exchange("pair", sent_o)
    all_hidden = exchange_dp([hidden] * parts)

    share = jax.ShapeDtypeStruct((rows, width // parts), BF16)
    results = call(
        functools.partial(backward_kernel, n, len(got_p), len(out_b), parts),
        fixed[:2] + [(dp, "smem")] + fixed[2:] + copy(slope, silu, *got_p),
        out_b + [share] * parts,
        expert_flops,
        weight_bytes,
        [
            pltpu.VMEM((rows, width), BF16),
            pltpu.VMEM((local, width, most), BF16),
            pltpu.VMEM((local, width, most), F32),
        ]
        + stream,
    )
    sent_b, shares = results[: len(out_b)], results[len(out_b) :]
    all_shares = exchange_dp(shares)
    if TIE_B == "hidden":
        sent_b = tie(list(sent_b), (all_hidden, got_o))
    if TIE_B == "both":
        sent_b = tie(sent_b, (all_hidden, all_shares))
    got_b = exchange("all", sent_b)

    part = call(
        part_kernel,
        [place] + copy(mix_mate, *got_o),
        jax.ShapeDtypeStruct(tokens.shape, BF16),
        total * tok_count * width // CHEAP,
        block_bytes // CHEAP,
    )

    def spread(pair, x, mix, given):
        out = jax.ShapeDtypeStruct(tokens.shape, BF16)
        return call(
            lambda copies, *refs: spread_kernel(copies, n, pair, *refs),
            [place] + copy(ids, weights, comp_scale, x, mix, *given),
            out,
            2 * total * tok_count * width // CHEAP,
            block_bytes // CHEAP,
            [pltpu.VMEM(out.shape, BF16), pltpu.SemaphoreType.DMA((HALVES,))],
            lazy=True,
            out_spec=HBM,
        )

    if TIE_S:
        part = tie(part, all_shares)
    part = from_mate(part)
    if not TIE_S:
        layer_output = spread(True, tokens, mix_own, [part, *got_o])
        all_shares = tie(all_shares, layer_output)
    grad_shape = jax.ShapeDtypeStruct((local, ff, width // parts), BF16)
    grad_down = call(
        functools.partial(grad_kernel, n, parts),
        [scalars, place] + copy(*all_hidden, *all_shares),
        grad_shape,
        2 * parts * rows * ff * local * width // parts,
        parts * rows * (ff + width // parts) * 2,
        [pltpu.VMEM(grad_shape.shape, BF16), pltpu.SemaphoreType.DMA((local,))],
        out_spec=HBM,
    )
    if TIE_S:
        layer_output = spread(True, tokens, tie(mix_own, grad_down), [part, *got_o])
    if TIE_G:
        mix_g = tie(mix_g, (layer_output, grad_down))
    grad_tokens = spread(False, cotangent, mix_g, got_b)
    return (layer_output, grad_tokens, grad_down)


def tie(x, after):
    return lax.optimization_barrier((x, after))[0]


def solution(mesh):
    token_spec = P(("dp", "expert"), None)
    weight_spec = P("expert", None, None)
    in_specs = (token_spec,) * 5 + (P(), P()) + (weight_spec,) * 3
    out_specs = (token_spec, token_spec, P("expert", None, "dp"))
    return jax.shard_map(
        on_device, mesh=mesh, in_specs=in_specs, out_specs=out_specs, check_vma=False
    )
```

```python
import functools

import jax
import jax.numpy as jnp
from jax import lax
from jax.experimental import pallas as pl
from jax.experimental.pallas import tpu as pltpu
from jax.sharding import PartitionSpec as P

PAIR_ROWS = 20
MOST = 16
HALVES = 2
BLOCK_ROWS = HALVES * PAIR_ROWS
CHUNK = 8
FF_TILE = 256
VMEM_LIMIT = 64 * 1024 * 1024 - 65536
EARLY = 1
SLOPE = jnp.bfloat16
TURN = 1
JOIN = True
TIE_O = ()
TIE_S = True
TIE_L = True
TIE_P = (4,)
NEAR = (2,)
ORDER_C = ()
MATE_FIRST = ()
CHEAP = 1000000
FIRST_P = False
TIE_B = "hidden"
TIE_G = True
F32 = jnp.float32
BF16 = jnp.bfloat16

NN = (((1,), (0,)), ((), ()))
NT = (((1,), (1,)), ((), ()))
TN = (((0,), (0,)), ((), ()))


def mm(a, b, dims=NN):
    return lax.dot_general(a, b, dims, preferred_element_type=F32)


def iota(shape, dim):
    return lax.broadcasted_iota(jnp.int32, shape, dim)


def places_of(ids, codes, counts_ref):
    count = jnp.zeros_like(ids)
    base = jnp.zeros_like(ids)
    for expert in range(counts_ref.shape[0]):
        hit = ids == expert
        count = jnp.where(hit, counts_ref[expert], count)
        if expert % 2:
            base = jnp.where(hit, counts_ref[expert - 1], base)
    laps = jnp.floor((codes.astype(F32) + 0.5) / count.astype(F32)).astype(jnp.int32)
    return ids >> 1, base + codes - laps * count


def membership(rows, total, values):
    picks, tokens = rows.shape
    index = iota((total, tokens), 0)
    parts = []
    for half in range(HALVES):
        part = jnp.zeros((total, tokens), F32)
        for pick in range(picks):
            hit = index == rows[pick : pick + 1, :] + half * PAIR_ROWS
            value = 1.0 if values is None else values[pick : pick + 1, :]
            part = jnp.where(hit, value, part)
        parts.append(part)
    return jnp.concatenate(parts, axis=1)


def split_halves(x):
    width = x.shape[1] // HALVES
    return jnp.concatenate([x[:, :width], x[:, width:]], axis=0)


def row_places(row, blocks):
    inside = jnp.floor((row.astype(F32) + 0.5) * (1.0 / blocks)).astype(jnp.int32)
    return (row - inside * blocks) * BLOCK_ROWS + inside


def unpack_rows(blocks):
    flat = jnp.concatenate(blocks, axis=0)
    count = len(blocks)
    rows = count * PAIR_ROWS
    shape = (rows, count * BLOCK_ROWS)
    place = row_places(iota(shape, 0), count)
    col = iota(shape, 1)
    picks = [(col == place + half * PAIR_ROWS).astype(F32) for half in range(HALVES)]
    out = mm(jnp.concatenate(picks, axis=0).astype(BF16), flat).astype(BF16)
    return jnp.concatenate([out[h * rows : (h + 1) * rows] for h in range(HALVES)], axis=1)


class Blocks:
    def __init__(self, refs, n, group):
        self.refs, self.n, self.group = refs, n, group

    def at(self, j):
        if len(self.refs) == self.n:
            return self.refs[j]
        if len(self.refs) > 1:
            return self.refs[j // 2].at[(j % 2) ^ (self.group & 1)]
        return self.refs[0].at[self.group ^ j]

    def load(self, start, stop):
        return [self.at(j)[...] for j in range(start, stop)]

    def store(self, start, flat):
        for j in range(flat.shape[0] // BLOCK_ROWS):
            self.at(start + j)[...] = flat[j * BLOCK_ROWS : (j + 1) * BLOCK_ROWS].astype(BF16)


def pack_windows(parts, n, c, size, counts_ref, group, dims):
    picks, pieces = [], []
    half = parts[0].shape[1 if dims == NN else 0] // HALVES
    for e, (x, (start, stop)) in enumerate(zip(parts, windows(n))):
        shape = (size * BLOCK_ROWS, stop - start)
        row = iota(shape, 0)
        index = iota(shape, 1) + start
        inside = jnp.floor((index.astype(F32) + 0.5) * (1.0 / n)).astype(jnp.int32)
        place = (index - inside * n - c) * BLOCK_ROWS + inside
        first = inside < counts_ref[2 * group]
        place = jnp.where(first if e == 0 else jnp.logical_not(first), place, -BLOCK_ROWS * n)
        if n > size:
            block = index - inside * n
            place = jnp.where((block >= c) & (block < c + size), place, -BLOCK_ROWS * n)
        for h in range(HALVES):
            picks.append((row == place + h * PAIR_ROWS).astype(F32).astype(BF16))
            span = slice(h * half, (h + 1) * half)
            pieces.append(x[:, span] if dims == NN else x[span, :])
    return mm(jnp.concatenate(picks, axis=1), jnp.concatenate(pieces, axis=0 if dims == NN else 1), dims)


def windows(n):
    return (0, MOST * n), ((PAIR_ROWS - MOST) * n, PAIR_ROWS * n)


def owned(e, start, stop, n, counts_ref, group):
    index = iota((stop - start, 1), 0) + start
    first = index < counts_ref[2 * group] * n
    return first if e == 0 else jnp.logical_not(first)


def gather_kernel(mean, n, group_ref, counts_ref, ids_ref, codes_ref, weights_ref, x_ref, *outs):
    group = group_ref[0]
    device, inside = places_of(ids_ref[...], codes_ref[...], counts_ref)
    rows = (device ^ group) * BLOCK_ROWS + inside
    member = membership(rows, n * BLOCK_ROWS, None if mean else weights_ref[...])
    sums = mm(member.astype(BF16), split_halves(x_ref[...]))
    if mean:
        sums = sums / jnp.maximum(jnp.sum(member, axis=1, keepdims=True), 1.0)
    Blocks(outs, n, group).store(0, sums)


def gather_pair_kernel(mean, n, group_ref, counts_ref, *refs):
    sources, outs = (refs[:4], refs[4:8]), refs[8:]
    group = group_ref[0]
    core = group & 1
    for mate, (ids_ref, codes_ref, weights_ref, x_ref) in enumerate(sources):
        rows = pair_rows(ids_ref, codes_ref, counts_ref, group)
        member = membership(rows, len(outs) * BLOCK_ROWS, None if mean else weights_ref[...])
        sums = mm(member.astype(BF16), split_halves(x_ref[...]))
        if mean:
            sums = sums / jnp.maximum(jnp.sum(member, axis=1, keepdims=True), 1.0)
        for d, out in enumerate(outs):
            out[core ^ mate] = sums[d * BLOCK_ROWS : (d + 1) * BLOCK_ROWS].astype(BF16)


def own_scale(scale_ref, group, e):
    row = iota(scale_ref.shape, 0)
    return jnp.sum(jnp.where(row == 2 * group + e, scale_ref[...].astype(F32), 0.0), axis=0, keepdims=True)


def gain_of(ids, weights, scale):
    experts, tokens = scale.shape[0], ids.shape[1]
    expert = iota((experts, tokens), 0)
    mix = jnp.zeros((experts, tokens), F32)
    for pick in range(ids.shape[0]):
        mix = jnp.where(expert == ids[pick : pick + 1, :], weights[pick : pick + 1, :], mix)
    high = mix.astype(BF16)
    low = (mix - high.astype(F32)).astype(BF16)
    return mm(high, scale, TN) + mm(low, scale, TN)


def pair_rows(ids_ref, codes_ref, counts_ref, group):
    device, inside = places_of(ids_ref[...], codes_ref[...], counts_ref)
    away = (device >> 1) ^ (group >> 1)
    return jnp.where((device & 1) == (group & 1), away * BLOCK_ROWS + inside, -BLOCK_ROWS)


def prepare_kernel(n, counts_ref, group_ref, ids_ref, codes_ref, weights_ref, *refs):
    mate, (mix_g_ref, mix_own_ref, mix_mate_ref) = refs[:-3], refs[-3:]
    device, inside = places_of(ids_ref[...], codes_ref[...], counts_ref)
    rows = (device ^ group_ref[0]) * BLOCK_ROWS + inside
    member = membership(rows, n * BLOCK_ROWS, None)
    divisor = jnp.maximum(jnp.sum(member, axis=1, keepdims=True), 1.0)
    mix_g_ref[...] = (member / divisor).T.astype(BF16)
    for out, (i, c, w) in ((mix_own_ref, (ids_ref, codes_ref, weights_ref)), (mix_mate_ref, mate)):
        rows = pair_rows(i, c, counts_ref, group_ref[0])
        out[...] = membership(rows, n // 2 * BLOCK_ROWS, w[...]).T.astype(BF16)


def part_kernel(group_ref, mix_ref, *refs):
    blocks, out_ref = refs[:-1], refs[-1]
    flat = jnp.concatenate([b[(group_ref[0] & 1) ^ 1] for b in blocks], axis=0)
    back = mm(mix_ref[...], flat)
    tokens, width = out_ref.shape
    half = width // HALVES
    for h in range(HALVES):
        out_ref[:, h * half : (h + 1) * half] = back[h * tokens : (h + 1) * tokens].astype(BF16)


def spread_kernel(copies, n, pair, group_ref, ids_ref, weights_ref, scale_ref, x_ref, mix_ref, *refs):
    out_hbm, out_ref, sem = refs[-3:]
    given = refs[:-3]
    waits = iter(sorted(copies))
    take = lambda count: [copies[next(waits)].wait() for _ in range(count)]
    group = group_ref[0]
    take(3)
    gain = gain_of(ids_ref[...], weights_ref[...], scale_ref[...])
    take(1)
    base = gain * x_ref[...].astype(F32)
    take(1 + len(given))
    if pair:
        part_ref, blocks = given[0], given[1:]
        base = base + part_ref[...].astype(F32)
        flat = jnp.concatenate([b[group & 1] for b in blocks], axis=0)
    else:
        flat = jnp.concatenate(Blocks(given, n, group).load(0, n), axis=0)
    tokens, width = out_ref.shape
    half = width // HALVES
    sends = []
    for h in range(HALVES):
        cols = pl.ds(h * half, half)
        back = mm(mix_ref[h * tokens : (h + 1) * tokens, :], flat)
        out_ref[:, h * half : (h + 1) * half] = (base[:, h * half : (h + 1) * half] + back).astype(BF16)
        sends.append(pltpu.make_async_copy(out_ref.at[:, cols], out_hbm.at[:, cols], sem.at[h]))
        sends[-1].start()
    for send in sends:
        send.wait()


class Weights:
    def __init__(self, hbm, vmem, sems):
        self.hbm, self.vmem, self.sems = hbm, vmem, sems
        self.per = vmem[0].shape[2] // FF_TILE
        self.steps = vmem[0].shape[0] * self.per

    def views(self, s):
        e = s // self.per
        cols = pl.ds(pl.multiple_of((s - e * self.per) * FF_TILE, FF_TILE), FF_TILE)
        return [(e, slice(None), cols)] * 2 + [(e, cols, slice(None))]

    def copies(self, s):
        return [
            pltpu.make_async_copy(h.at[view], v.at[view], self.sems.at[s, i])
            for i, (h, v, view) in enumerate(zip(self.hbm, self.vmem, self.views(s)))
        ]

    def start(self, s):
        for copy in self.copies(s):
            copy.start()

    def run(self, body):
        for e in range(self.vmem[0].shape[0]):

            def step(f, carry):
                s = e * self.per + f

                for copy in self.copies(s):
                    copy.wait()
                cols = pl.ds(pl.multiple_of(f * FF_TILE, FF_TILE), FF_TILE)
                body(e, cols, *[v.at[view] for v, view in zip(self.vmem, self.views(s))])
                return carry

            lax.fori_loop(0, self.per, step, 0)


def start_weights(refs):
    first = next(i for i, ref in enumerate(refs) if ref.shape == refs[-4].shape)
    weights = Weights(refs[first : first + 3], refs[-4:-1], refs[-1])
    for s in range(EARLY):
        weights.start(s)


def unpack_all(x_ref, blocks, n):
    size = min(CHUNK, n)
    for c in range(0, n, size):
        part = unpack_rows(blocks.load(c, c + size))
        if n == size:
            x_ref[...] = part
        else:
            for r in range(PAIR_ROWS):
                x_ref[r * n + c : r * n + c + size, :] = part[r * size : (r + 1) * size]


def forward_kernel(n, n_in, n_out, counts_ref, group_ref, scale_ref, wg_hbm, wu_hbm, wd_hbm, *refs):
    group = group_ref[0]
    blocks, outs = Blocks(refs[:n_in], n, group), Blocks(refs[n_in : n_in + n_out], n, group)
    hidden_ref, slope_ref, silu_ref, x_ref, acc_ref, wg_ref, wu_ref, wd_ref, sems = refs[n_in + n_out :]
    weights = Weights((wg_hbm, wu_hbm, wd_hbm), (wg_ref, wu_ref, wd_ref), sems)
    for s in range(EARLY, weights.steps):
        weights.start(s)
    unpack_all(x_ref, blocks, n)
    hidden_ref[...] = jnp.zeros_like(hidden_ref)
    for e, (start, stop) in enumerate(windows(n)):
        scale = own_scale(scale_ref, group, e)
        acc_ref[e] = -(scale * x_ref[start:stop, :].astype(F32))

    def body(e, cols, wg, wu, wd):
        start, stop = windows(n)[e]
        mine = owned(e, start, stop, n, counts_ref, group)
        x = x_ref[start:stop, :]
        gate = mm(x, wg[...])
        up = mm(x, wu[...])
        sg = 1.0 / (1.0 + jnp.exp(-gate))
        silu = gate * sg
        hidden = (silu * up).astype(BF16)
        slope = up * sg * (1.0 + gate * (1.0 - sg))
        acc_ref[e] += mm(hidden, wd[...])
        hidden_ref[start:stop, cols] = jnp.where(mine, hidden, hidden_ref[start:stop, cols])
        slope_ref[e, cols, :] = slope.T.astype(SLOPE)
        silu_ref[e, cols, :] = silu.T.astype(SLOPE)

    weights.run(body)
    size = min(n, CHUNK)
    parts = [acc_ref[e].astype(BF16) for e in range(2)]
    for c in range(0, n, size):
        outs.store(c, pack_windows(parts, n, c, size, counts_ref, group, NN))


def backward_kernel(n, n_in, n_out, parts, counts_ref, group_ref, dp_ref, scale_ref, wg_hbm, wu_hbm, wd_hbm, slope_ref, silu_ref, *refs):
    group = group_ref[0]
    blocks, outs = Blocks(refs[:n_in], n, group), Blocks(refs[n_in : n_in + n_out], n, group)
    refs = refs[n_in + n_out :]
    shares, (pull_ref, turned_ref, acc_ref, wg_ref, wu_ref, wd_ref, sems) = refs[:parts], refs[parts:]
    weights = Weights((wg_hbm, wu_hbm, wd_hbm), (wg_ref, wu_ref, wd_ref), sems)
    for s in range(EARLY, weights.steps):
        weights.start(s)
    unpack_all(pull_ref, blocks, n)
    for e, (start, stop) in enumerate(windows(n)):
        if TURN == 1:
            turned_ref[e] = pull_ref[start:stop, :].T
            scale = jnp.broadcast_to(own_scale(scale_ref, group, e), (8, pull_ref.shape[1])).T[:, :1]
            acc_ref[e] = -(scale * turned_ref[e].astype(F32))
        else:
            pull = pull_ref[start:stop, :].astype(F32)
            turned_ref[e] = pull.T.astype(BF16)
            acc_ref[e] = -(own_scale(scale_ref, group, e) * pull).T
    width = pull_ref.shape[1] // parts
    for k, share in enumerate(shares):
        start = pl.multiple_of((dp_ref[0] ^ k) * width, width)
        share[...] = pull_ref[:, pl.ds(start, width)]

    def body(e, cols, wg, wu, wd):
        d_hidden = mm(wd[...], turned_ref[e])
        d_gate = (d_hidden * slope_ref[e, cols, :].astype(F32)).astype(BF16)
        d_up = (d_hidden * silu_ref[e, cols, :].astype(F32)).astype(BF16)
        if JOIN:
            both = jnp.concatenate([wg[...], wu[...]], axis=1)
            acc_ref[e] += mm(both, jnp.concatenate([d_gate, d_up], axis=0))
        else:
            acc_ref[e] += mm(wg[...], d_gate) + mm(wu[...], d_up)

    weights.run(body)
    size = min(n, CHUNK)
    sums = [acc_ref[e].astype(BF16) for e in range(2)]
    for c in range(0, n, size):
        outs.store(c, pack_windows(sums, n, c, size, counts_ref, group, NT))


def grad_kernel(n, parts, counts_ref, group_ref, *refs):
    hidden, shares = refs[:parts], refs[parts : 2 * parts]
    out_hbm, out_ref, sem = refs[2 * parts :]
    sends = []
    for e in range(2):
        start, stop = windows(n)[e]
        mine = owned(e, start, stop, n, counts_ref, group_ref[0])
        h_all = jnp.concatenate([h[start:stop, :] for h in hidden], axis=0)
        pull = jnp.concatenate(
            [jnp.where(mine, s[start:stop, :].astype(F32), 0.0).astype(BF16) for s in shares], axis=0
        )
        out_ref[e] = mm(h_all, pull, TN).astype(BF16)
        sends.append(pltpu.make_async_copy(out_ref.at[e], out_hbm.at[e], sem.at[e]))
        sends[-1].start()
    for send in sends:
        send.wait()


SMEM = pl.BlockSpec(memory_space=pltpu.SMEM)
VMEM = pl.BlockSpec(memory_space=pltpu.VMEM)
HBM = pl.BlockSpec(memory_space=pltpu.HBM)


def call(kernel, ins, outs, flops, nbytes, scratch=(), lazy=False, early=None, out_spec=VMEM):
    arrays, specs, buffers = [], [], []
    for x, way in ins:
        if way in ("copy", "scalars", "stay"):
            x = pltpu.with_memory_space_constraint(x, pltpu.HBM)
        if way == "copy":
            buffers.append(pltpu.VMEM(x.shape, x.dtype))
        if way == "scalars":
            buffers.append(pltpu.SMEM(x.shape, x.dtype))
        arrays.append(x)
        specs.append(SMEM if way == "smem" else HBM)
    copied = [i for i, (_, way) in enumerate(ins) if way in ("copy", "scalars")]
    buffers.append(pltpu.SemaphoreType.DMA((max(len(copied), 1),)))

    def body(*refs):
        refs = list(refs)
        given, sems = refs[len(refs) - len(buffers) : -1], refs[-1]
        refs = refs[: len(refs) - len(buffers)]
        copies = {i: pltpu.make_async_copy(refs[i], given[k], sems.at[k]) for k, i in enumerate(copied)}
        for copy in copies.values():
            copy.start()
        if early is not None:
            early(refs)
        for k, i in enumerate(copied):
            refs[i] = given[k]
        if lazy:
            kernel(copies, *refs)
        else:
            for copy in copies.values():
                copy.wait()
            kernel(*refs)

    return pl.pallas_call(
        body,
        out_shape=outs,
        in_specs=specs,
        out_specs=jax.tree.map(lambda _: out_spec, outs),
        scratch_shapes=list(scratch) + buffers,
        compiler_params=pltpu.CompilerParams(vmem_limit_bytes=VMEM_LIMIT),
        cost_estimate=pl.CostEstimate(flops=flops, bytes_accessed=nbytes, transcendentals=0),
    )(*arrays)


def on_device(
    tokens, expert_ids, bucket_codes, route_weights, cotangent, counts, comp_scale, w_gate, w_up, w_down
):
    tok_count, width = tokens.shape
    n = lax.axis_size("expert")
    parts = lax.axis_size("dp")
    local, _, ff = w_gate.shape
    expert_total = counts.shape[0]
    half = width // HALVES
    rows = n * PAIR_ROWS
    total = n * BLOCK_ROWS
    most = n * MOST
    group = lax.axis_index("expert").astype(jnp.int32).reshape(1)
    dp = lax.axis_index("dp").astype(jnp.int32).reshape(1)
    ids, codes, weights = expert_ids.T, bucket_codes.T, route_weights.T
    block_bytes = total * width
    picks = ids.shape[0]

    block = (BLOCK_ROWS, half)

    def layout(way):
        if way == "permute":
            return [jax.ShapeDtypeStruct(block, BF16)] * n
        if way == "pair":
            return [jax.ShapeDtypeStruct((2, *block), BF16)] * (n // 2)
        return [jax.ShapeDtypeStruct((n, *block), BF16)]

    def exchange(way, values):
        if way == "all":
            return [lax.all_to_all(values[0], "expert", split_axis=0, concat_axis=0, tiled=True)]
        step = n // len(values)
        got = {0: values[0]}
        for d in sorted(range(1, len(values)), key=lambda d: (d not in ORDER_C, ORDER_C.index(d) if d in ORDER_C else d)):
            got[d] = lax.ppermute(values[d], "expert", [(i, i ^ (step * d)) for i in range(n)])
        return [got[d] for d in range(len(values))]

    def from_mate(x):
        return lax.ppermute(x, "expert", [(i, i ^ 1) for i in range(n)])

    def exchange_dp(values):
        return [values[0]] + [
            lax.ppermute(values[k], "dp", [(i, i ^ k) for i in range(parts)]) for k in range(1, parts)
        ]

    scalars = (counts, "scalars")
    place = (group, "smem")
    copy = lambda *xs: [(x, "copy") for x in xs]
    vmem = lambda xs: [(x, "vmem") for x in xs]

    mate = [from_mate(v).T for v in (expert_ids, bucket_codes, route_weights)]

    def gather(mean, way, x):
        kernel, given = gather_kernel, [ids, codes, weights, x]
        if way == "pair":
            kernel, given = gather_pair_kernel, given + mate + [from_mate(x)]
        return call(
            functools.partial(kernel, mean, n),
            [place, scalars] + copy(*given),
            layout(way),
            2 * total * tok_count * width,
            block_bytes,
        )

    sent_c = list(gather(True, "permute", tokens))
    sent_p = list(gather(False, "pair", tie(cotangent, sent_c[0])))
    if NEAR:
        near = [sent_c[k] for k in NEAR]
        for k, v in zip(NEAR, tie(near, sent_p)):
            sent_c[k] = v
    if MATE_FIRST:
        for k, v in zip(MATE_FIRST, tie([sent_c[k] for k in MATE_FIRST], mate[0])):
            sent_c[k] = v
    got_c = exchange("permute", sent_c)
    if FIRST_P:
        early = lax.ppermute(sent_p[1], "expert", [(i, i ^ 2) for i in range(n)])
        late = tie(sent_p[2:], ([got_c[k] for k in TIE_P], early))
        got_p = [sent_p[0], early] + [
            lax.ppermute(v, "expert", [(i, i ^ (2 * d)) for i in range(n)]) for d, v in enumerate(late, 2)
        ]
    else:
        sent_p = tie(sent_p, [got_c[k] for k in TIE_P])
        got_p = exchange("pair", sent_p)

    weight_bytes = 3 * local * width * ff * 2
    expert_flops = 2 * 3 * rows * local * width * ff
    out_o, out_b = layout("pair"), layout("all")
    stream = [
        pltpu.VMEM(w_gate.shape, BF16),
        pltpu.VMEM(w_up.shape, BF16),
        pltpu.VMEM(w_down.shape, BF16),
        pltpu.SemaphoreType.DMA((local * ff // FF_TILE, 3)),
    ]
    fixed = [scalars, place] + copy(comp_scale) + [(w, "stay") for w in (w_gate, w_up, w_down)]

    results = call(
        functools.partial(forward_kernel, n, len(got_c), len(out_o)),
        fixed + copy(*got_c),
        out_o
        + [
            jax.ShapeDtypeStruct((rows, ff), BF16),
            jax.ShapeDtypeStruct((local, ff, most), SLOPE),
            jax.ShapeDtypeStruct((local, ff, most), SLOPE),
        ],
        expert_flops,
        weight_bytes,
        [pltpu.VMEM((rows, width), BF16), pltpu.VMEM((local, most, width), F32)] + stream,
        early=start_weights,
    )
    mix = jax.ShapeDtypeStruct((HALVES * tok_count, total), BF16)
    mix_pair = jax.ShapeDtypeStruct((HALVES * tok_count, total // 2), BF16)
    mix_g, mix_own, mix_mate = call(
        functools.partial(prepare_kernel, n),
        [scalars, place] + copy(tie(ids, results[0]), codes, weights, *mate),
        [mix, mix_pair, mix_pair],
        0,
        3 * tok_count * total * 4 // CHEAP,
    )
    sent_o, (hidden, slope, silu) = results[: len(out_o)], results[len(out_o) :]
    if TIE_O:
        sent_o = tie(list(sent_o), [got_p[d] for d in TIE_O])
    got_o = exchange("pair", sent_o)
    all_hidden = exchange_dp([hidden] * parts)

    share = jax.ShapeDtypeStruct((rows, width // parts), BF16)
    results = call(
        functools.partial(backward_kernel, n, len(got_p), len(out_b), parts),
        fixed[:2] + [(dp, "smem")] + fixed[2:] + copy(slope, silu, *got_p),
        out_b + [share] * parts,
        expert_flops,
        weight_bytes,
        [
            pltpu.VMEM((rows, width), BF16),
            pltpu.VMEM((local, width, most), BF16),
            pltpu.VMEM((local, width, most), F32),
        ]
        + stream,
        early=start_weights,
    )
    sent_b, shares = results[: len(out_b)], results[len(out_b) :]
    all_shares = exchange_dp(shares)
    if TIE_B == "hidden":
        sent_b = tie(list(sent_b), (all_hidden, got_o))
    if TIE_B == "both":
        sent_b = tie(sent_b, (all_hidden, all_shares))
    got_b = exchange("all", sent_b)

    part = call(
        part_kernel,
        [place] + copy(mix_mate, *got_o),
        jax.ShapeDtypeStruct(tokens.shape, BF16),
        total * tok_count * width // CHEAP,
        block_bytes // CHEAP,
    )

    def spread(pair, x, mix, given):
        out = jax.ShapeDtypeStruct(tokens.shape, BF16)
        return call(
            lambda copies, *refs: spread_kernel(copies, n, pair, *refs),
            [place] + copy(ids, weights, comp_scale, x, mix, *given),
            out,
            2 * total * tok_count * width // CHEAP,
            block_bytes // CHEAP,
            [pltpu.VMEM(out.shape, BF16), pltpu.SemaphoreType.DMA((HALVES,))],
            lazy=True,
            out_spec=HBM,
        )

    if TIE_S:
        part = tie(part, all_shares)
    part = from_mate(part)
    if not TIE_S:
        layer_output = spread(True, tokens, mix_own, [part, *got_o])
        all_shares = tie(all_shares, layer_output)
    grad_shape = jax.ShapeDtypeStruct((local, ff, width // parts), BF16)
    grad_down = call(
        functools.partial(grad_kernel, n, parts),
        [scalars, place] + copy(*all_hidden, *all_shares),
        grad_shape,
        2 * parts * rows * ff * local * width // parts,
        parts * rows * (ff + width // parts) * 2,
        [pltpu.VMEM(grad_shape.shape, BF16), pltpu.SemaphoreType.DMA((local,))],
        out_spec=HBM,
    )
    if TIE_S:
        layer_output = spread(True, tokens, tie(mix_own, grad_down), [part, *got_o])
    if TIE_G:
        mix_g = tie(mix_g, (layer_output, grad_down))
    grad_tokens = spread(False, cotangent, mix_g, got_b)
    return (layer_output, grad_tokens, grad_down)


def tie(x, after):
    return lax.optimization_barrier((x, after))[0]


def solution(mesh):
    token_spec = P(("dp", "expert"), None)
    weight_spec = P("expert", None, None)
    in_specs = (token_spec,) * 5 + (P(), P()) + (weight_spec,) * 3
    out_specs = (token_spec, token_spec, P("expert", None, "dp"))
    return jax.shard_map(
        on_device, mesh=mesh, in_specs=in_specs, out_specs=out_specs, check_vma=False
    )
```

```python
import functools

import jax
import jax.numpy as jnp
from jax import lax
from jax.experimental import pallas as pl
from jax.experimental.pallas import tpu as pltpu
from jax.sharding import PartitionSpec as P

PAIR_ROWS = 20
MOST = 16
HALVES = 2
BLOCK_ROWS = HALVES * PAIR_ROWS
CHUNK = 8
FF_TILE = 256
VMEM_LIMIT = 64 * 1024 * 1024 - 65536
EARLY = 1
SLOPE = jnp.bfloat16
TURN = 1
JOIN = True
TIE_O = ()
TIE_S = True
TIE_L = True
TIE_P = (4,)
NEAR = (2,)
ORDER_C = ()
MATE_FIRST = ()
CHEAP = 1000000
FIRST_P = False
TIE_B = "hidden"
TIE_G = True
F32 = jnp.float32
BF16 = jnp.bfloat16

NN = (((1,), (0,)), ((), ()))
NT = (((1,), (1,)), ((), ()))
TN = (((0,), (0,)), ((), ()))


def mm(a, b, dims=NN):
    return lax.dot_general(a, b, dims, preferred_element_type=F32)


def iota(shape, dim):
    return lax.broadcasted_iota(jnp.int32, shape, dim)


def places_of(ids, codes, counts_ref):
    count = jnp.zeros_like(ids)
    base = jnp.zeros_like(ids)
    for expert in range(counts_ref.shape[0]):
        hit = ids == expert
        count = jnp.where(hit, counts_ref[expert], count)
        if expert % 2:
            base = jnp.where(hit, counts_ref[expert - 1], base)
    laps = jnp.floor((codes.astype(F32) + 0.5) / count.astype(F32)).astype(jnp.int32)
    return ids >> 1, base + codes - laps * count


def membership(rows, total, values):
    picks, tokens = rows.shape
    index = iota((total, tokens), 0)
    parts = []
    for half in range(HALVES):
        part = jnp.zeros((total, tokens), F32)
        for pick in range(picks):
            hit = index == rows[pick : pick + 1, :] + half * PAIR_ROWS
            value = 1.0 if values is None else values[pick : pick + 1, :]
            part = jnp.where(hit, value, part)
        parts.append(part)
    return jnp.concatenate(parts, axis=1)


def split_halves(x):
    width = x.shape[1] // HALVES
    return jnp.concatenate([x[:, :width], x[:, width:]], axis=0)


def row_places(row, blocks):
    inside = jnp.floor((row.astype(F32) + 0.5) * (1.0 / blocks)).astype(jnp.int32)
    return (row - inside * blocks) * BLOCK_ROWS + inside


def unpack_rows(blocks):
    flat = jnp.concatenate(blocks, axis=0)
    count = len(blocks)
    rows = count * PAIR_ROWS
    shape = (rows, count * BLOCK_ROWS)
    place = row_places(iota(shape, 0), count)
    col = iota(shape, 1)
    picks = [(col == place + half * PAIR_ROWS).astype(F32) for half in range(HALVES)]
    out = mm(jnp.concatenate(picks, axis=0).astype(BF16), flat).astype(BF16)
    return jnp.concatenate([out[h * rows : (h + 1) * rows] for h in range(HALVES)], axis=1)


class Blocks:
    def __init__(self, refs, n, group):
        self.refs, self.n, self.group = refs, n, group

    def at(self, j):
        if len(self.refs) == self.n:
            return self.refs[j]
        if len(self.refs) > 1:
            return self.refs[j // 2].at[(j % 2) ^ (self.group & 1)]
        return self.refs[0].at[self.group ^ j]

    def load(self, start, stop):
        return [self.at(j)[...] for j in range(start, stop)]

    def store(self, start, flat):
        for j in range(flat.shape[0] // BLOCK_ROWS):
            self.at(start + j)[...] = flat[j * BLOCK_ROWS : (j + 1) * BLOCK_ROWS].astype(BF16)


def pack_windows(parts, n, c, size, counts_ref, group, dims):
    picks, pieces = [], []
    half = parts[0].shape[1 if dims == NN else 0] // HALVES
    for e, (x, (start, stop)) in enumerate(zip(parts, windows(n))):
        shape = (size * BLOCK_ROWS, stop - start)
        row = iota(shape, 0)
        index = iota(shape, 1) + start
        inside = jnp.floor((index.astype(F32) + 0.5) * (1.0 / n)).astype(jnp.int32)
        place = (index - inside * n - c) * BLOCK_ROWS + inside
        first = inside < counts_ref[2 * group]
        place = jnp.where(first if e == 0 else jnp.logical_not(first), place, -BLOCK_ROWS * n)
        if n > size:
            block = index - inside * n
            place = jnp.where((block >= c) & (block < c + size), place, -BLOCK_ROWS * n)
        for h in range(HALVES):
            picks.append((row == place + h * PAIR_ROWS).astype(F32).astype(BF16))
            span = slice(h * half, (h + 1) * half)
            pieces.append(x[:, span] if dims == NN else x[span, :])
    return mm(jnp.concatenate(picks, axis=1), jnp.concatenate(pieces, axis=0 if dims == NN else 1), dims)


def windows(n):
    return (0, MOST * n), ((PAIR_ROWS - MOST) * n, PAIR_ROWS * n)


def owned(e, start, stop, n, counts_ref, group):
    index = iota((stop - start, 1), 0) + start
    first = index < counts_ref[2 * group] * n
    return first if e == 0 else jnp.logical_not(first)


def gather_kernel(mean, n, group_ref, counts_ref, ids_ref, codes_ref, weights_ref, x_ref, *outs):
    group = group_ref[0]
    device, inside = places_of(ids_ref[...], codes_ref[...], counts_ref)
    rows = (device ^ group) * BLOCK_ROWS + inside
    member = membership(rows, n * BLOCK_ROWS, None if mean else weights_ref[...])
    sums = mm(member.astype(BF16), split_halves(x_ref[...]))
    if mean:
        sums = sums / jnp.maximum(jnp.sum(member, axis=1, keepdims=True), 1.0)
    Blocks(outs, n, group).store(0, sums)


def gather_pair_kernel(mean, n, group_ref, counts_ref, *refs):
    sources, outs = (refs[:4], refs[4:8]), refs[8:]
    group = group_ref[0]
    core = group & 1
    for mate, (ids_ref, codes_ref, weights_ref, x_ref) in enumerate(sources):
        rows = pair_rows(ids_ref, codes_ref, counts_ref, group)
        member = membership(rows, len(outs) * BLOCK_ROWS, None if mean else weights_ref[...])
        sums = mm(member.astype(BF16), split_halves(x_ref[...]))
        if mean:
            sums = sums / jnp.maximum(jnp.sum(member, axis=1, keepdims=True), 1.0)
        for d, out in enumerate(outs):
            out[core ^ mate] = sums[d * BLOCK_ROWS : (d + 1) * BLOCK_ROWS].astype(BF16)


def own_scale(scale_ref, group, e):
    row = iota(scale_ref.shape, 0)
    return jnp.sum(jnp.where(row == 2 * group + e, scale_ref[...].astype(F32), 0.0), axis=0, keepdims=True)


def gain_of(ids, weights, scale):
    experts, tokens = scale.shape[0], ids.shape[1]
    expert = iota((experts, tokens), 0)
    mix = jnp.zeros((experts, tokens), F32)
    for pick in range(ids.shape[0]):
        mix = jnp.where(expert == ids[pick : pick + 1, :], weights[pick : pick + 1, :], mix)
    high = mix.astype(BF16)
    low = (mix - high.astype(F32)).astype(BF16)
    return mm(high, scale, TN) + mm(low, scale, TN)


def pair_rows(ids_ref, codes_ref, counts_ref, group):
    device, inside = places_of(ids_ref[...], codes_ref[...], counts_ref)
    away = (device >> 1) ^ (group >> 1)
    return jnp.where((device & 1) == (group & 1), away * BLOCK_ROWS + inside, -BLOCK_ROWS)


def prepare_kernel(n, counts_ref, group_ref, ids_ref, codes_ref, weights_ref, *refs):
    mate, (mix_g_ref, mix_own_ref, mix_mate_ref) = refs[:-3], refs[-3:]
    device, inside = places_of(ids_ref[...], codes_ref[...], counts_ref)
    rows = (device ^ group_ref[0]) * BLOCK_ROWS + inside
    member = membership(rows, n * BLOCK_ROWS, None)
    divisor = jnp.maximum(jnp.sum(member, axis=1, keepdims=True), 1.0)
    mix_g_ref[...] = (member / divisor).T.astype(BF16)
    for out, (i, c, w) in ((mix_own_ref, (ids_ref, codes_ref, weights_ref)), (mix_mate_ref, mate)):
        rows = pair_rows(i, c, counts_ref, group_ref[0])
        out[...] = membership(rows, n // 2 * BLOCK_ROWS, w[...]).T.astype(BF16)


def part_kernel(group_ref, mix_ref, *refs):
    blocks, out_ref = refs[:-1], refs[-1]
    flat = jnp.concatenate([b[(group_ref[0] & 1) ^ 1] for b in blocks], axis=0)
    back = mm(mix_ref[...], flat)
    tokens, width = out_ref.shape
    half = width // HALVES
    for h in range(HALVES):
        out_ref[:, h * half : (h + 1) * half] = back[h * tokens : (h + 1) * tokens].astype(BF16)


def spread_kernel(copies, n, pair, group_ref, ids_ref, weights_ref, scale_ref, x_ref, mix_ref, *refs):
    out_hbm, out_ref, sem = refs[-3:]
    given = refs[:-3]
    waits = iter(sorted(copies))
    take = lambda count: [copies[next(waits)].wait() for _ in range(count)]
    group = group_ref[0]
    take(3)
    gain = gain_of(ids_ref[...], weights_ref[...], scale_ref[...])
    take(1)
    base = gain * x_ref[...].astype(F32)
    take(1 + len(given))
    if pair:
        part_ref, blocks = given[0], given[1:]
        base = base + part_ref[...].astype(F32)
        flat = jnp.concatenate([b[group & 1] for b in blocks], axis=0)
    else:
        flat = jnp.concatenate(Blocks(given, n, group).load(0, n), axis=0)
    tokens, width = out_ref.shape
    half = width // HALVES
    sends = []
    for h in range(HALVES):
        cols = pl.ds(h * half, half)
        back = mm(mix_ref[h * tokens : (h + 1) * tokens, :], flat)
        out_ref[:, h * half : (h + 1) * half] = (base[:, h * half : (h + 1) * half] + back).astype(BF16)
        sends.append(pltpu.make_async_copy(out_ref.at[:, cols], out_hbm.at[:, cols], sem.at[h]))
        sends[-1].start()
    for send in sends:
        send.wait()


class Weights:
    def __init__(self, hbm, vmem, sems):
        self.hbm, self.vmem, self.sems = hbm, vmem, sems
        self.per = vmem[0].shape[2] // FF_TILE
        self.steps = vmem[0].shape[0] * self.per

    def views(self, s):
        e = s // self.per
        cols = pl.ds(pl.multiple_of((s - e * self.per) * FF_TILE, FF_TILE), FF_TILE)
        return [(e, slice(None), cols)] * 2 + [(e, cols, slice(None))]

    def copies(self, s):
        return [
            pltpu.make_async_copy(h.at[view], v.at[view], self.sems.at[s, i])
            for i, (h, v, view) in enumerate(zip(self.hbm, self.vmem, self.views(s)))
        ]

    def start(self, s):
        for copy in self.copies(s):
            copy.start()

    def run(self, body):
        for e in range(self.vmem[0].shape[0]):

            def step(f, carry):
                s = e * self.per + f

                for copy in self.copies(s):
                    copy.wait()
                cols = pl.ds(pl.multiple_of(f * FF_TILE, FF_TILE), FF_TILE)
                body(e, cols, *[v.at[view] for v, view in zip(self.vmem, self.views(s))])
                return carry

            lax.fori_loop(0, self.per, step, 0)


def start_weights(refs):
    first = next(i for i, ref in enumerate(refs) if ref.shape == refs[-4].shape)
    weights = Weights(refs[first : first + 3], refs[-4:-1], refs[-1])
    for s in range(EARLY):
        weights.start(s)


def unpack_all(x_ref, blocks, n):
    size = min(CHUNK, n)
    for c in range(0, n, size):
        part = unpack_rows(blocks.load(c, c + size))
        if n == size:
            x_ref[...] = part
        else:
            for r in range(PAIR_ROWS):
                x_ref[r * n + c : r * n + c + size, :] = part[r * size : (r + 1) * size]


def forward_kernel(n, n_in, n_out, counts_ref, group_ref, scale_ref, wg_hbm, wu_hbm, wd_hbm, *refs):
    group = group_ref[0]
    blocks, outs = Blocks(refs[:n_in], n, group), Blocks(refs[n_in : n_in + n_out], n, group)
    hidden_ref, slope_ref, silu_ref, x_ref, acc_ref, wg_ref, wu_ref, wd_ref, sems = refs[n_in + n_out :]
    weights = Weights((wg_hbm, wu_hbm, wd_hbm), (wg_ref, wu_ref, wd_ref), sems)
    for s in range(EARLY, weights.steps):
        weights.start(s)
    unpack_all(x_ref, blocks, n)
    hidden_ref[...] = jnp.zeros_like(hidden_ref)
    for e, (start, stop) in enumerate(windows(n)):
        scale = own_scale(scale_ref, group, e)
        acc_ref[e] = -(scale * x_ref[start:stop, :].astype(F32))

    def body(e, cols, wg, wu, wd):
        start, stop = windows(n)[e]
        mine = owned(e, start, stop, n, counts_ref, group)
        x = x_ref[start:stop, :]
        gate = mm(x, wg[...])
        up = mm(x, wu[...])
        sg = 1.0 / (1.0 + jnp.exp(-gate))
        silu = gate * sg
        hidden = (silu * up).astype(BF16)
        slope = up * sg * (1.0 + gate * (1.0 - sg))
        acc_ref[e] += mm(hidden, wd[...])
        hidden_ref[start:stop, cols] = jnp.where(mine, hidden, hidden_ref[start:stop, cols])
        slope_ref[e, cols, :] = slope.T.astype(SLOPE)
        silu_ref[e, cols, :] = silu.T.astype(SLOPE)

    weights.run(body)
    size = min(n, CHUNK)
    parts = [acc_ref[e].astype(BF16) for e in range(2)]
    for c in range(0, n, size):
        outs.store(c, pack_windows(parts, n, c, size, counts_ref, group, NN))


def backward_kernel(n, n_in, n_out, parts, counts_ref, group_ref, dp_ref, scale_ref, wg_hbm, wu_hbm, wd_hbm, slope_ref, silu_ref, *refs):
    group = group_ref[0]
    blocks, outs = Blocks(refs[:n_in], n, group), Blocks(refs[n_in : n_in + n_out], n, group)
    refs = refs[n_in + n_out :]
    shares, (pull_ref, turned_ref, acc_ref, share_sems, wg_ref, wu_ref, wd_ref, sems) = refs[:parts], refs[parts:]
    weights = Weights((wg_hbm, wu_hbm, wd_hbm), (wg_ref, wu_ref, wd_ref), sems)
    for s in range(weights.steps):
        weights.start(s)
    unpack_all(pull_ref, blocks, n)
    for e, (start, stop) in enumerate(windows(n)):
        if TURN == 1:
            turned_ref[e] = pull_ref[start:stop, :].T
            scale = jnp.broadcast_to(own_scale(scale_ref, group, e), (8, pull_ref.shape[1])).T[:, :1]
            acc_ref[e] = -(scale * turned_ref[e].astype(F32))
        else:
            pull = pull_ref[start:stop, :].astype(F32)
            turned_ref[e] = pull.T.astype(BF16)
            acc_ref[e] = -(own_scale(scale_ref, group, e) * pull).T
    width = pull_ref.shape[1] // parts
    sends = []
    for k, share in enumerate(shares):
        start = pl.multiple_of((dp_ref[0] ^ k) * width, width)
        sends.append(pltpu.make_async_copy(pull_ref.at[:, pl.ds(start, width)], share, share_sems.at[k]))
        sends[-1].start()

    def body(e, cols, wg, wu, wd):
        d_hidden = mm(wd[...], turned_ref[e])
        d_gate = (d_hidden * slope_ref[e, cols, :].astype(F32)).astype(BF16)
        d_up = (d_hidden * silu_ref[e, cols, :].astype(F32)).astype(BF16)
        if JOIN:
            both = jnp.concatenate([wg[...], wu[...]], axis=1)
            acc_ref[e] += mm(both, jnp.concatenate([d_gate, d_up], axis=0))
        else:
            acc_ref[e] += mm(wg[...], d_gate) + mm(wu[...], d_up)

    weights.run(body)
    size = min(n, CHUNK)
    sums = [acc_ref[e].astype(BF16) for e in range(2)]
    for c in range(0, n, size):
        outs.store(c, pack_windows(sums, n, c, size, counts_ref, group, NT))
    for send in sends:
        send.wait()


def grad_kernel(n, parts, counts_ref, group_ref, *refs):
    hidden, shares = refs[:parts], refs[parts : 2 * parts]
    out_hbm, out_ref, sem = refs[2 * parts :]
    sends = []
    for e in range(2):
        start, stop = windows(n)[e]
        mine = owned(e, start, stop, n, counts_ref, group_ref[0])
        h_all = jnp.concatenate([h[start:stop, :] for h in hidden], axis=0)
        pull = jnp.concatenate(
            [jnp.where(mine, s[start:stop, :].astype(F32), 0.0).astype(BF16) for s in shares], axis=0
        )
        out_ref[e] = mm(h_all, pull, TN).astype(BF16)
        sends.append(pltpu.make_async_copy(out_ref.at[e], out_hbm.at[e], sem.at[e]))
        sends[-1].start()
    for send in sends:
        send.wait()


SMEM = pl.BlockSpec(memory_space=pltpu.SMEM)
VMEM = pl.BlockSpec(memory_space=pltpu.VMEM)
HBM = pl.BlockSpec(memory_space=pltpu.HBM)


def call(kernel, ins, outs, flops, nbytes, scratch=(), lazy=False, early=None, out_spec=VMEM):
    arrays, specs, buffers = [], [], []
    for x, way in ins:
        if way in ("copy", "scalars", "stay"):
            x = pltpu.with_memory_space_constraint(x, pltpu.HBM)
        if way == "copy":
            buffers.append(pltpu.VMEM(x.shape, x.dtype))
        if way == "scalars":
            buffers.append(pltpu.SMEM(x.shape, x.dtype))
        arrays.append(x)
        specs.append(SMEM if way == "smem" else HBM)
    copied = [i for i, (_, way) in enumerate(ins) if way in ("copy", "scalars")]
    buffers.append(pltpu.SemaphoreType.DMA((max(len(copied), 1),)))

    def body(*refs):
        refs = list(refs)
        given, sems = refs[len(refs) - len(buffers) : -1], refs[-1]
        refs = refs[: len(refs) - len(buffers)]
        copies = {i: pltpu.make_async_copy(refs[i], given[k], sems.at[k]) for k, i in enumerate(copied)}
        for copy in copies.values():
            copy.start()
        if early is not None:
            early(refs)
        for k, i in enumerate(copied):
            refs[i] = given[k]
        if lazy:
            kernel(copies, *refs)
        else:
            for copy in copies.values():
                copy.wait()
            kernel(*refs)

    return pl.pallas_call(
        body,
        out_shape=outs,
        in_specs=specs,
        out_specs=out_spec if isinstance(out_spec, list) else jax.tree.map(lambda _: out_spec, outs),
        scratch_shapes=list(scratch) + buffers,
        compiler_params=pltpu.CompilerParams(vmem_limit_bytes=VMEM_LIMIT),
        cost_estimate=pl.CostEstimate(flops=flops, bytes_accessed=nbytes, transcendentals=0),
    )(*arrays)


def on_device(
    tokens, expert_ids, bucket_codes, route_weights, cotangent, counts, comp_scale, w_gate, w_up, w_down
):
    tok_count, width = tokens.shape
    n = lax.axis_size("expert")
    parts = lax.axis_size("dp")
    local, _, ff = w_gate.shape
    expert_total = counts.shape[0]
    half = width // HALVES
    rows = n * PAIR_ROWS
    total = n * BLOCK_ROWS
    most = n * MOST
    group = lax.axis_index("expert").astype(jnp.int32).reshape(1)
    dp = lax.axis_index("dp").astype(jnp.int32).reshape(1)
    ids, codes, weights = expert_ids.T, bucket_codes.T, route_weights.T
    block_bytes = total * width
    picks = ids.shape[0]

    block = (BLOCK_ROWS, half)

    def layout(way):
        if way == "permute":
            return [jax.ShapeDtypeStruct(block, BF16)] * n
        if way == "pair":
            return [jax.ShapeDtypeStruct((2, *block), BF16)] * (n // 2)
        return [jax.ShapeDtypeStruct((n, *block), BF16)]

    def exchange(way, values):
        if way == "all":
            return [lax.all_to_all(values[0], "expert", split_axis=0, concat_axis=0, tiled=True)]
        step = n // len(values)
        got = {0: values[0]}
        for d in sorted(range(1, len(values)), key=lambda d: (d not in ORDER_C, ORDER_C.index(d) if d in ORDER_C else d)):
            got[d] = lax.ppermute(values[d], "expert", [(i, i ^ (step * d)) for i in range(n)])
        return [got[d] for d in range(len(values))]

    def from_mate(x):
        return lax.ppermute(x, "expert", [(i, i ^ 1) for i in range(n)])

    def exchange_dp(values):
        return [values[0]] + [
            lax.ppermute(values[k], "dp", [(i, i ^ k) for i in range(parts)]) for k in range(1, parts)
        ]

    scalars = (counts, "scalars")
    place = (group, "smem")
    copy = lambda *xs: [(x, "copy") for x in xs]
    vmem = lambda xs: [(x, "vmem") for x in xs]

    mate = [from_mate(v).T for v in (expert_ids, bucket_codes, route_weights)]

    def gather(mean, way, x):
        kernel, given = gather_kernel, [ids, codes, weights, x]
        if way == "pair":
            kernel, given = gather_pair_kernel, given + mate + [from_mate(x)]
        return call(
            functools.partial(kernel, mean, n),
            [place, scalars] + copy(*given),
            layout(way),
            2 * total * tok_count * width,
            block_bytes,
        )

    sent_c = list(gather(True, "permute", tokens))
    sent_p = list(gather(False, "pair", tie(cotangent, sent_c[0])))
    if NEAR:
        near = [sent_c[k] for k in NEAR]
        for k, v in zip(NEAR, tie(near, sent_p)):
            sent_c[k] = v
    if MATE_FIRST:
        for k, v in zip(MATE_FIRST, tie([sent_c[k] for k in MATE_FIRST], mate[0])):
            sent_c[k] = v
    got_c = exchange("permute", sent_c)
    if FIRST_P:
        early = lax.ppermute(sent_p[1], "expert", [(i, i ^ 2) for i in range(n)])
        late = tie(sent_p[2:], ([got_c[k] for k in TIE_P], early))
        got_p = [sent_p[0], early] + [
            lax.ppermute(v, "expert", [(i, i ^ (2 * d)) for i in range(n)]) for d, v in enumerate(late, 2)
        ]
    else:
        sent_p = tie(sent_p, [got_c[k] for k in TIE_P])
        got_p = exchange("pair", sent_p)

    weight_bytes = 3 * local * width * ff * 2
    expert_flops = 2 * 3 * rows * local * width * ff
    out_o, out_b = layout("pair"), layout("all")
    stream = [
        pltpu.VMEM(w_gate.shape, BF16),
        pltpu.VMEM(w_up.shape, BF16),
        pltpu.VMEM(w_down.shape, BF16),
        pltpu.SemaphoreType.DMA((local * ff // FF_TILE, 3)),
    ]
    fixed = [scalars, place] + copy(comp_scale) + [(w, "stay") for w in (w_gate, w_up, w_down)]

    results = call(
        functools.partial(forward_kernel, n, len(got_c), len(out_o)),
        fixed + copy(*got_c),
        out_o
        + [
            jax.ShapeDtypeStruct((rows, ff), BF16),
            jax.ShapeDtypeStruct((local, ff, most), SLOPE),
            jax.ShapeDtypeStruct((local, ff, most), SLOPE),
        ],
        expert_flops,
        weight_bytes,
        [pltpu.VMEM((rows, width), BF16), pltpu.VMEM((local, most, width), F32)] + stream,
        early=start_weights,
    )
    mix = jax.ShapeDtypeStruct((HALVES * tok_count, total), BF16)
    mix_pair = jax.ShapeDtypeStruct((HALVES * tok_count, total // 2), BF16)
    mix_g, mix_own, mix_mate = call(
        functools.partial(prepare_kernel, n),
        [scalars, place] + copy(tie(ids, results[0]), codes, weights, *mate),
        [mix, mix_pair, mix_pair],
        0,
        3 * tok_count * total * 4 // CHEAP,
    )
    sent_o, (hidden, slope, silu) = results[: len(out_o)], results[len(out_o) :]
    if TIE_O:
        sent_o = tie(list(sent_o), [got_p[d] for d in TIE_O])
    got_o = exchange("pair", sent_o)
    all_hidden = exchange_dp([hidden] * parts)

    share = jax.ShapeDtypeStruct((rows, width // parts), BF16)
    results = call(
        functools.partial(backward_kernel, n, len(got_p), len(out_b), parts),
        fixed[:2] + [(dp, "smem")] + fixed[2:] + copy(slope, silu, *got_p),
        out_b + [share] * parts,
        expert_flops,
        weight_bytes,
        [
            pltpu.VMEM((rows, width), BF16),
            pltpu.VMEM((local, width, most), BF16),
            pltpu.VMEM((local, width, most), F32),
            pltpu.SemaphoreType.DMA((parts,)),
        ]
        + stream,
        out_spec=[VMEM] * len(out_b) + [HBM] * parts,
    )
    sent_b, shares = results[: len(out_b)], results[len(out_b) :]
    all_shares = exchange_dp(shares)
    if TIE_B == "hidden":
        sent_b = tie(list(sent_b), (all_hidden, got_o))
    if TIE_B == "both":
        sent_b = tie(sent_b, (all_hidden, all_shares))
    got_b = exchange("all", sent_b)

    part = call(
        part_kernel,
        [place] + copy(mix_mate, *got_o),
        jax.ShapeDtypeStruct(tokens.shape, BF16),
        total * tok_count * width // CHEAP,
        block_bytes // CHEAP,
    )

    def spread(pair, x, mix, given):
        out = jax.ShapeDtypeStruct(tokens.shape, BF16)
        return call(
            lambda copies, *refs: spread_kernel(copies, n, pair, *refs),
            [place] + copy(ids, weights, comp_scale, x, mix, *given),
            out,
            2 * total * tok_count * width // CHEAP,
            block_bytes // CHEAP,
            [pltpu.VMEM(out.shape, BF16), pltpu.SemaphoreType.DMA((HALVES,))],
            lazy=True,
            out_spec=HBM,
        )

    if TIE_S:
        part = tie(part, all_shares)
    part = from_mate(part)
    if not TIE_S:
        layer_output = spread(True, tokens, mix_own, [part, *got_o])
        all_shares = tie(all_shares, layer_output)
    grad_shape = jax.ShapeDtypeStruct((local, ff, width // parts), BF16)
    grad_down = call(
        functools.partial(grad_kernel, n, parts),
        [scalars, place] + copy(*all_hidden, *all_shares),
        grad_shape,
        2 * parts * rows * ff * local * width // parts,
        parts * rows * (ff + width // parts) * 2,
        [pltpu.VMEM(grad_shape.shape, BF16), pltpu.SemaphoreType.DMA((local,))],
        out_spec=HBM,
    )
    if TIE_S:
        layer_output = spread(True, tokens, tie(mix_own, grad_down), [part, *got_o])
    if TIE_G:
        mix_g = tie(mix_g, (layer_output, grad_down))
    grad_tokens = spread(False, cotangent, mix_g, got_b)
    return (layer_output, grad_tokens, grad_down)


def tie(x, after):
    return lax.optimization_barrier((x, after))[0]


def solution(mesh):
    token_spec = P(("dp", "expert"), None)
    weight_spec = P("expert", None, None)
    in_specs = (token_spec,) * 5 + (P(), P()) + (weight_spec,) * 3
    out_specs = (token_spec, token_spec, P("expert", None, "dp"))
    return jax.shard_map(
        on_device, mesh=mesh, in_specs=in_specs, out_specs=out_specs, check_vma=False
    )
```
